256 devices in a mesh: batch: 2 (over x_lo), ctx: 32 (over z, y), tp: 4 (over x_hi, core).
Axes of the slice: x: 4 (x_hi: 2, x_lo: 2; x = x_hi * 2 + x_lo), y: 4, z: 8, core: 2. Of those that a mesh axis runs over, the one named last changes fastest.
Arguments:
- frames: bfloat16 [12288, 1536], P(('batch', 'ctx'), 'tp'), parts along dimension 0, may hold values from -6 to 6
- attn_gain: float32 [1536], replicated, may hold values from 0.5 to 1.5
- query_key_value: bfloat16 [3, 1536, 1536], P(None, None, 'tp'), may hold values from -1 to 1
- out_weight: bfloat16 [1536, 1536], P('tp'), may hold values from -6 to 6
- conv_gain: float32 [1536], replicated, may hold values from 0.5 to 1.5
- glu_weight: bfloat16 [2, 1536, 1536], P(None, None, 'tp'), may hold values from -0.15625 to 0.15625
- depth_kernel: bfloat16 [31, 1536], P(None, 'tp'), may hold values from -1 to 1
- depth_bias: float32 [1536], P('tp'), may hold values from -4 to 4
- proj_weight: bfloat16 [1536, 1536], P('tp'), may hold values from -0.15625 to 0.15625
Outputs:
- layer_out: bfloat16 [12288, 1536], P(('batch', 'ctx'), 'tp'), parts along dimension 0
The draws below stay inside these ranges and needn't reach their ends.
There are 2 independent parts, one for each index of `batch`. The reference program is written for one: setup_inputs(seed, part) draws one part's arguments, and reference() takes and returns one part's arrays. A program takes and returns all parts, laid end to end along the dimension named above; an argument that names none is the same for every part. Nothing has to cross between parts.
All inputs are finite; a program needn't handle non-finite values.
Results may differ from the reference program's by a relative error of at most 0.019.
Values may be sent and summed in bfloat16 or wider, within the bound.
No kernel may reach another device: no remote copies, remote signals or barrier semaphores. Data moves between devices by JAX's collectives and lax.ppermute only.
A program may use at most 128 MiB of HBM per device.

```python
import math
import jax
import jax.numpy as jnp
from jax import lax

D = 1536
HEADS = 16
HEAD = 96
KERNEL = 31
FRAMES = 6144


def draw_query_key_value(key, part):
    key = jax.random.fold_in(key, 11)
    first_key = jax.random.fold_in(key, 0)
    base = jax.random.normal(first_key, (3, D, D), jnp.float32) / math.sqrt(D)
    return jnp.clip(base, -1.0, 1.0).astype(jnp.bfloat16)


def shard_levels(key, shape, cuts, least, high):
    loudness = 1.0
    for position, blocks in cuts:
        heights = jax.random.uniform(jax.random.fold_in(jax.random.fold_in(key, 6), position), (blocks,), jnp.float32, least / len(cuts), high / len(cuts))
        loudness = loudness * jnp.repeat(jnp.exp(heights), shape[position] // blocks).reshape((-1,) + (1,) * (len(shape) - 1 - position))
    return loudness


def noise(key, shape, deviation, most, shards=(), kind=jnp.bfloat16):
    level = shard_levels(key, shape, shards, -0.22, 0.18) if shards else 1.0
    entries = jax.random.normal(key, shape, jnp.float32) * deviation * level
    return jnp.minimum(jnp.maximum(entries, -most), most).astype(kind)


def setup_inputs(seed: int = 0, part: int = 0) -> dict:
    seeds = jax.random.split(jax.random.key(seed), 10)
    part_splits = jax.random.split(jax.random.fold_in(seeds[9], part), 10)
    return {
        "frames": noise(part_splits[0], (FRAMES, D), 1.0, 6.0, ((0, 32), (1, 4))),
        "attn_gain": jnp.clip(jax.random.uniform(seeds[1], (D,), jnp.float32, 0.5, 1.5), 0.5, 1.5),
        "query_key_value": draw_query_key_value(jax.random.fold_in(seeds[9], 71), part),
        "out_weight": noise(seeds[3], (D, D), 1.0, 6.0, ((0, 4),)),
        "conv_gain": jnp.clip(jax.random.uniform(seeds[4], (D,), jnp.float32, 0.5, 1.5), 0.5, 1.5),
        "glu_weight": noise(seeds[5], (2, D, D), D ** -0.5, 0.15625, ((2, 4),)),
        "depth_kernel": noise(seeds[6], (KERNEL, D), KERNEL ** -0.5, 1.0, ((1, 4),)),
        "depth_bias": noise(seeds[7], (D,), 1.0, 4.0, ((0, 4),), jnp.float32),
        "proj_weight": noise(seeds[8], (D, D), D ** -0.5, 0.15625, ((0, 4),)),
    }


def layer_norm(inputs, gain):
    inputs = inputs.astype(jnp.float32)
    average = lax.optimization_barrier(jnp.mean(inputs, axis=-1, keepdims=True))
    centered = inputs - average
    variance = lax.optimization_barrier(jnp.mean(centered * centered, axis=-1, keepdims=True))
    return (centered * lax.rsqrt(variance + 1e-05) * gain.astype(jnp.float32)).astype(jnp.bfloat16)

def reference(frames, attn_gain, query_key_value, out_weight, conv_gain, glu_weight, depth_kernel, depth_bias, proj_weight):
    normed = layer_norm(frames, attn_gain)
    queries = jnp.dot(normed, query_key_value[0], preferred_element_type=jnp.float32).astype(jnp.bfloat16)
    key_rows = jnp.dot(normed, query_key_value[1], preferred_element_type=jnp.float32).astype(jnp.bfloat16)
    value_rows = jnp.dot(normed, query_key_value[2], preferred_element_type=jnp.float32).astype(jnp.bfloat16)
    query_heads = queries.reshape(FRAMES, HEADS, HEAD).astype(jnp.float32)
    key_heads = key_rows.reshape(FRAMES, HEADS, HEAD).astype(jnp.float32)
    value_heads = value_rows.reshape(FRAMES, HEADS, HEAD).astype(jnp.float32)
    score_scale = 1.0 / math.sqrt(HEAD)
    block_len = math.gcd(FRAMES, 256)

    def attend(start):
        query_block = lax.dynamic_slice_in_dim(query_heads, start, block_len, 0)
        scores = jnp.einsum('qhd,khd->hqk', query_block, key_heads) * score_scale
        row_max = lax.optimization_barrier(jnp.max(scores, axis=-1, keepdims=True))
        weights = jnp.exp(scores - row_max)
        denominator = lax.optimization_barrier(jnp.sum(weights, axis=-1))
        rounded = weights.astype(jnp.bfloat16).astype(jnp.float32)
        summed = jnp.einsum('hqk,khd->qhd', rounded, value_heads)
        return (summed / jnp.transpose(denominator)[:, :, None]).astype(jnp.bfloat16)
    starts = jnp.arange(FRAMES // block_len, dtype=jnp.int32) * block_len
    context = lax.map(attend, starts).reshape(FRAMES, D)
    attended = jnp.dot(context, out_weight, preferred_element_type=jnp.float32)
    middle = (frames.astype(jnp.float32) + attended).astype(jnp.bfloat16)
    normed_conv = layer_norm(middle, conv_gain)
    value_half = jnp.dot(normed_conv, glu_weight[0], preferred_element_type=jnp.float32)
    gate_half = jnp.dot(normed_conv, glu_weight[1], preferred_element_type=jnp.float32)
    glu = (value_half * jax.nn.sigmoid(gate_half)).astype(jnp.bfloat16)
    reach = KERNEL // 2
    padded = jnp.pad(glu.astype(jnp.float32), ((reach, reach), (0, 0)))
    convolved = jnp.zeros((FRAMES, D), jnp.float32)
    for kernel_tap in range(KERNEL):
        convolved = convolved + padded[kernel_tap:kernel_tap + FRAMES] * depth_kernel[kernel_tap].astype(jnp.float32)
    activated = jax.nn.silu(convolved + depth_bias.astype(jnp.float32)).astype(jnp.bfloat16)
    projected = jnp.dot(activated, proj_weight, preferred_element_type=jnp.float32)
    return (middle.astype(jnp.float32) + projected).astype(jnp.bfloat16)
```

```python
import functools
import math

import jax
import jax.numpy as jnp
from jax import lax
from jax.experimental import pallas as pl
from jax.experimental.pallas import tpu as pltpu
from jax.sharding import Mesh
from jax.sharding import PartitionSpec as P

D = 1536
HEAD = 96
HEADS_HERE = 4
COLS = 384
ROWS = 192
REACH = 15
HALO = 16
EXT = 512
TP = ("xh", "core")
CTX = ("z", "y")
Q_SCALE = math.log2(math.e) / math.sqrt(HEAD)
VMEM_LIMIT = 40 * 2**20


def layer_norm(inputs, gain):
    inputs = inputs.astype(jnp.float32)
    average = jnp.mean(inputs, axis=-1, keepdims=True)
    centered = inputs - average
    variance = jnp.mean(centered * centered, axis=-1, keepdims=True)
    return (centered * lax.rsqrt(variance + 1e-05) * gain).astype(jnp.bfloat16)


def split_three(value):
    high = value.astype(jnp.bfloat16).astype(jnp.float32)
    rest = value - high
    mid = rest.astype(jnp.bfloat16).astype(jnp.float32)
    return high, mid, rest - mid


def head_window(head):
    start = 0 if head < 2 else 128
    lane = lax.broadcasted_iota(jnp.int32, (1, 256), 1) + start
    return start, (lane >= head * HEAD) & (lane < (head + 1) * HEAD)


def attention_kernel(q_ref, k_ref, v_ref, o_ref):
    tile = q_ref.shape[0]
    total = jnp.zeros((tile, COLS), jnp.float32)
    lane = lax.broadcasted_iota(jnp.int32, (1, 128), 1)
    stats = jnp.zeros((tile, 128), jnp.float32)
    for head in range(HEADS_HERE):
        start, inside = head_window(head)
        queries = jnp.where(inside, q_ref[:, start : start + 256], 0)
        scores = lax.dot_general(
            queries,
            k_ref[:, start : start + 256],
            (((1,), (1,)), ((), ())),
            preferred_element_type=jnp.float32,
        )
        top = jnp.max(scores, axis=1, keepdims=True)
        weights = jnp.exp2(scores - top)
        denominator = jnp.sum(weights, axis=1, keepdims=True)
        summed = jnp.dot(
            weights.astype(jnp.bfloat16),
            v_ref[:, start : start + 256],
            preferred_element_type=jnp.float32,
        )
        part = jnp.where(inside, summed * (1.0 / denominator), 0.0)
        blank = jnp.zeros((tile, 128), jnp.float32)
        total = total + jnp.concatenate([part, blank] if start == 0 else [blank, part], 1)
        for place, piece in enumerate(split_three(top + jnp.log2(denominator))):
            stats = jnp.where(lane == place * HEADS_HERE + head, piece, stats)
    o_ref[:, :COLS] = total.astype(jnp.bfloat16)
    o_ref[:, COLS:] = stats.astype(jnp.bfloat16)


def attention(queries, keys_values, tile):
    count = queries.shape[0]
    key_count = keys_values.shape[0]
    return pl.pallas_call(
        attention_kernel,
        grid=(count // tile,),
        in_specs=[
            pl.BlockSpec((tile, COLS), lambda i: (i, 0)),
            pl.BlockSpec((key_count, COLS), lambda i: (0, 0)),
            pl.BlockSpec((key_count, COLS), lambda i: (0, 1)),
        ],
        out_specs=pl.BlockSpec((tile, EXT), lambda i: (i, 0)),
        out_shape=jax.ShapeDtypeStruct((count, EXT), jnp.bfloat16),
        compiler_params=pltpu.CompilerParams(vmem_limit_bytes=VMEM_LIMIT),
        name="attention",
    )(queries, keys_values, keys_values)


def combine_kernel(parts_ref, o_ref):
    count = parts_ref.shape[0]
    lane = lax.broadcasted_iota(jnp.int32, (1, COLS), 1)
    logs = []
    for part in range(count):
        stats = parts_ref[part, :, COLS:].astype(jnp.float32)
        logs.append(stats[:, 0:4] + stats[:, 4:8] + stats[:, 8:12])
    top = functools.reduce(jnp.maximum, logs)
    shares = [jnp.exp2(log - top) for log in logs]
    inverse = 1.0 / functools.reduce(jnp.add, shares)
    total = jnp.zeros((parts_ref.shape[1], COLS), jnp.float32)
    for part in range(count):
        share = shares[part] * inverse
        spread = jnp.zeros((parts_ref.shape[1], COLS), jnp.float32)
        for head in range(HEADS_HERE):
            inside = (lane >= head * HEAD) & (lane < (head + 1) * HEAD)
            spread = jnp.where(inside, share[:, head : head + 1], spread)
        total = total + spread * parts_ref[part, :, :COLS].astype(jnp.float32)
    o_ref[...] = total.astype(jnp.bfloat16)


def combine(parts):
    return pl.pallas_call(
        combine_kernel,
        out_shape=jax.ShapeDtypeStruct((parts.shape[1], COLS), jnp.bfloat16),
        compiler_params=pltpu.CompilerParams(vmem_limit_bytes=VMEM_LIMIT),
        name="combine",
    )(parts)


def middle_kernel(place_ref, rows_ref, context_ref, w0, w1, w2, w3, gain_ref, glu_ref, m_ref, g_ref):
    place = place_ref[0]
    total = rows_ref[...].astype(jnp.float32)
    for offset, weight in enumerate((w0, w1, w2, w3)):
        total = total + jnp.dot(
            context_ref[place ^ offset], weight[...], preferred_element_type=jnp.float32
        )
    middle = total.astype(jnp.bfloat16)
    for position in range(4):

        @pl.when(place == position)
        def _():
            m_ref[...] = middle[:, position * COLS : (position + 1) * COLS]

    normed = layer_norm(middle, gain_ref[...])
    value = jnp.dot(normed, glu_ref[0], preferred_element_type=jnp.float32)
    gate = jnp.dot(normed, glu_ref[1], preferred_element_type=jnp.float32)
    g_ref[...] = (value * (1.0 / (1.0 + jnp.exp(-gate)))).astype(jnp.bfloat16)


def middle_and_glu(place, rows, context, weights, gain, glu_weight):
    count = rows.shape[0]
    vmem = pl.BlockSpec(memory_space=pltpu.VMEM)
    return pl.pallas_call(
        middle_kernel,
        in_specs=[pl.BlockSpec(memory_space=pltpu.SMEM)] + [vmem] * 8,
        out_specs=[vmem] * 2,
        out_shape=[jax.ShapeDtypeStruct((count, COLS), jnp.bfloat16)] * 2,
        compiler_params=pltpu.CompilerParams(vmem_limit_bytes=VMEM_LIMIT),
        name="middle",
    )(place, rows, context, *weights, gain.reshape(1, D), glu_weight)


def depthwise_kernel(before_ref, glu_ref, after_ref, taps_ref, bias_ref, o_ref, held):
    held[:HALO] = before_ref[...].astype(jnp.float32)
    held[HALO : HALO + ROWS] = glu_ref[...].astype(jnp.float32)
    held[HALO + ROWS :] = after_ref[...].astype(jnp.float32)
    taps = taps_ref[...].astype(jnp.float32)
    for column in range(COLS // 128):
        here = slice(column * 128, (column + 1) * 128)
        total = jnp.zeros((ROWS, 128), jnp.float32) + bias_ref[:, here]
        for tap in range(2 * REACH + 1):
            begin = HALO - REACH + tap
            total = total + held[begin : begin + ROWS, here] * taps[tap : tap + 1, here]
        o_ref[:, here] = (total / (1.0 + jnp.exp(-total))).astype(jnp.bfloat16)


def depthwise(before, glu, after, taps, bias):
    return pl.pallas_call(
        depthwise_kernel,
        out_shape=jax.ShapeDtypeStruct((ROWS, COLS), jnp.bfloat16),
        scratch_shapes=[pltpu.VMEM((ROWS + 2 * HALO, COLS), jnp.float32)],
        compiler_params=pltpu.CompilerParams(vmem_limit_bytes=VMEM_LIMIT),
        name="depthwise",
    )(before, glu, after, taps, bias.reshape(1, COLS))


def per_device(
    frames,
    attn_gain,
    query_key_value,
    out_weight,
    conv_gain,
    glu_weight,
    depth_kernel,
    depth_bias,
    proj_weight,
):
    place = lax.axis_index(TP)
    whole_rows = lax.all_gather(frames, TP, axis=1, tiled=True)
    normed = layer_norm(whole_rows, attn_gain)

    def project(index):
        return jnp.dot(normed, query_key_value[index], preferred_element_type=jnp.float32)

    keys_values = jnp.concatenate(
        [project(1).astype(jnp.bfloat16), project(2).astype(jnp.bfloat16)], axis=1
    )
    queries = (project(0) * Q_SCALE).astype(jnp.bfloat16)
    keys_values = lax.all_gather(keys_values, "z", axis=0, tiled=True)
    queries = lax.all_gather(queries, "y", axis=0, tiled=True)

    out_here, proj_here, queries = lax.optimization_barrier((out_weight, proj_weight, queries))
    swap = [(0, 1), (1, 0)]
    out_far = lax.ppermute(out_here, "xh", swap)
    out_core = lax.ppermute(out_here, "core", swap)
    out_far_core = lax.ppermute(out_far, "core", swap)
    out_pieces = (out_here, out_core, out_far, out_far_core)
    proj_split = proj_here.reshape(COLS, 4, COLS)
    proj_pieces = [lax.dynamic_index_in_dim(proj_split, place, 1, False)]
    for offset in range(1, 4):
        piece = lax.dynamic_index_in_dim(proj_split, place ^ offset, 1, False)
        proj_pieces.append(lax.ppermute(piece, TP, [(i, i ^ offset) for i in range(4)]))

    partial = attention(queries, keys_values, 256)
    parts = lax.all_to_all(partial, "y", split_axis=0, concat_axis=0, tiled=True)
    context = combine(parts.reshape(4, ROWS, EXT))
    context = lax.all_gather(context, TP, axis=0, tiled=False)
    middle, glu = middle_and_glu(
        place.reshape(1), whole_rows, context, out_pieces, conv_gain, glu_weight
    )
    before = lax.ppermute(glu[ROWS - HALO :], CTX, [(i, i + 1) for i in range(31)])
    after = lax.ppermute(glu[:HALO], CTX, [(i + 1, i) for i in range(31)])
    activated = depthwise(before, glu, after, depth_kernel, depth_bias)
    activated = lax.all_gather(activated, TP, axis=0, tiled=False)
    conv_sum = jnp.zeros((ROWS, COLS), jnp.float32)
    for offset in range(4):
        piece = lax.dynamic_index_in_dim(activated, place ^ offset, 0, False)
        conv_sum = conv_sum + jnp.dot(
            piece, proj_pieces[offset], preferred_element_type=jnp.float32
        )
    return (middle.astype(jnp.float32) + conv_sum).astype(jnp.bfloat16)


def solution(mesh):
    parted = Mesh(mesh.devices.reshape(2, 8, 4, 2, 2), ("batch", "z", "y", "xh", "core"))
    in_specs = (
        P(("batch",) + CTX, TP),
        P(),
        P(None, None, TP),
        P(TP, None),
        P(),
        P(None, None, TP),
        P(None, TP),
        P(TP),
        P(TP, None),
    )
    out_specs = P(("batch",) + CTX, TP)
    return jax.shard_map(
        per_device, mesh=parted, in_specs=in_specs, out_specs=out_specs, check_vma=False
    )
```

```python
import functools
import math

import jax
import jax.numpy as jnp
from jax import lax
from jax.experimental import pallas as pl
from jax.experimental.pallas import tpu as pltpu
from jax.sharding import Mesh
from jax.sharding import PartitionSpec as P

D = 1536
HEAD = 96
HEADS_HERE = 4
COLS = 384
ROWS = 192
REACH = 15
HALO = 16
EXT = 512
TP = ("xh", "core")
CTX = ("z", "y")
Q_SCALE = math.log2(math.e) / math.sqrt(HEAD)
VMEM_LIMIT = 24 * 2**20
VMEM_WHOLE = 60 * 2**20


def layer_norm(inputs, gain):
    inputs = inputs.astype(jnp.float32)
    average = jnp.mean(inputs, axis=-1, keepdims=True)
    centered = inputs - average
    variance = jnp.mean(centered * centered, axis=-1, keepdims=True)
    return (centered * lax.rsqrt(variance + 1e-05) * gain).astype(jnp.bfloat16)


def split_three(value):
    high = value.astype(jnp.bfloat16).astype(jnp.float32)
    rest = value - high
    mid = rest.astype(jnp.bfloat16).astype(jnp.float32)
    return high, mid, rest - mid


def head_window(head):
    start = 0 if head < 2 else 128
    lane = lax.broadcasted_iota(jnp.int32, (1, 256), 1) + start
    return start, (lane >= head * HEAD) & (lane < (head + 1) * HEAD)


def attend(queries, keys, values, head):
    start, inside = head_window(head)
    masked = jnp.where(inside, queries[:, start : start + 256], 0)
    window = jnp.concatenate([block[:, start : start + 256] for block in keys], 0)
    scores = lax.dot_general(
        masked, window, (((1,), (1,)), ((), ())), preferred_element_type=jnp.float32
    )
    top = jnp.max(scores, axis=1, keepdims=True)
    weights = jnp.exp2(scores - top)
    denominator = jnp.sum(weights, axis=1, keepdims=True)
    window = jnp.concatenate([block[:, start : start + 256] for block in values], 0)
    summed = jnp.dot(weights.astype(jnp.bfloat16), window, preferred_element_type=jnp.float32)
    return inside, summed, top, denominator


def widen(part, head):
    blank = jnp.zeros((part.shape[0], 128), jnp.float32)
    return jnp.concatenate([part, blank] if head < 2 else [blank, part], 1)


def split_refs(refs, count):
    keys = [ref.at[:, :COLS] for ref in refs[:count]]
    values = [ref.at[:, COLS:] for ref in refs[:count]]
    return keys, values, refs[count:]


def first_attention_kernel(blocks, *refs):
    pieces, refs = refs[: -blocks - 3], refs[-blocks - 3 :]
    keys, values, rest = split_refs(refs, blocks)
    o_ref, top_ref, sum_ref = rest
    lane = lax.broadcasted_iota(jnp.int32, (1, 128), 1)
    queries = jnp.concatenate([ref[...] for ref in pieces], 0)
    total = jnp.zeros((2 * ROWS, COLS), jnp.float32)
    tops = jnp.zeros((2 * ROWS, 128), jnp.float32)
    sums = jnp.ones((2 * ROWS, 128), jnp.float32)
    for head in range(HEADS_HERE):
        inside, summed, top, denominator = attend(queries, keys, values, head)
        total = total + widen(jnp.where(inside, summed, 0.0), head)
        tops = jnp.where(lane == head, top, tops)
        sums = jnp.where(lane == head, denominator, sums)
    o_ref[...] = total
    top_ref[...] = tops
    sum_ref[...] = sums


def last_attention_kernel(blocks, *refs):
    pieces, refs = refs[: -blocks - 5], refs[-blocks - 5 :]
    keys, values, rest = split_refs(refs, blocks)
    prior_ref, top_ref, sum_ref, *outs = rest
    lane = lax.broadcasted_iota(jnp.int32, (1, 128), 1)
    queries = jnp.concatenate([ref[...] for ref in pieces], 0)
    tops = jnp.zeros((2 * ROWS, 128), jnp.float32)
    sums = jnp.zeros((2 * ROWS, 128), jnp.float32)
    products = []
    for head in range(HEADS_HERE):
        inside, summed, top, denominator = attend(queries, keys, values, head)
        products.append((inside, summed))
        tops = jnp.where(lane == head, top, tops)
        sums = jnp.where(lane == head, denominator, sums)
    joint = jnp.maximum(tops, top_ref[...])
    rescale = jnp.exp2(tops - joint)
    prior_rescale = jnp.exp2(top_ref[...] - joint)
    denominator = sums * rescale + sum_ref[...] * prior_rescale
    inverse = 1.0 / denominator
    rescale = rescale * inverse
    prior_rescale = prior_rescale * inverse
    total = jnp.zeros((2 * ROWS, COLS), jnp.float32)
    for head, (inside, summed) in enumerate(products):
        start = 0 if head < 2 else 128
        part = (
            summed * rescale[:, head : head + 1]
            + prior_ref[:, start : start + 256] * prior_rescale[:, head : head + 1]
        )
        total = total + widen(jnp.where(inside, part, 0.0), head)
    high, mid, low = split_three(joint + jnp.log2(denominator))
    stats = jnp.where(
        lane < 4, high, jnp.where(lane < 8, pltpu.roll(mid, 4, 1), pltpu.roll(low, 8, 1))
    )
    for side in range(2):
        rows = slice(side * ROWS, (side + 1) * ROWS)
        outs[side][:, :COLS] = total[rows].astype(jnp.bfloat16)
        outs[side][:, COLS:] = stats[rows].astype(jnp.bfloat16)


def attention_cost(rows, blocks):
    flops = 2 * 2 * rows * ROWS * blocks * 256 * HEADS_HERE
    return pl.CostEstimate(flops=flops, bytes_accessed=4 * 2**20, transcendentals=0)


def first_attention(queries, blocks):
    rows = 2 * ROWS
    return pl.pallas_call(
        functools.partial(first_attention_kernel, len(blocks)),
        out_shape=[
            jax.ShapeDtypeStruct((rows, COLS), jnp.float32),
            jax.ShapeDtypeStruct((rows, 128), jnp.float32),
            jax.ShapeDtypeStruct((rows, 128), jnp.float32),
        ],
        compiler_params=pltpu.CompilerParams(vmem_limit_bytes=VMEM_LIMIT),
        cost_estimate=attention_cost(rows, len(blocks)),
        name="first_attention",
    )(*queries, *blocks)


def last_attention(queries, blocks, prior):
    return pl.pallas_call(
        functools.partial(last_attention_kernel, len(blocks)),
        out_shape=[jax.ShapeDtypeStruct((ROWS, EXT), jnp.bfloat16)] * 2,
        compiler_params=pltpu.CompilerParams(vmem_limit_bytes=VMEM_LIMIT),
        cost_estimate=attention_cost(2 * ROWS, len(blocks)),
        name="last_attention",
    )(*queries, *blocks, *prior)


def combine_kernel(*refs):
    parts, o_ref = refs[:-1], refs[-1]
    count = len(parts)
    lane = lax.broadcasted_iota(jnp.int32, (1, COLS), 1)
    logs = []
    for part in range(count):
        stats = parts[part][:, COLS:].astype(jnp.float32)
        logs.append(stats[:, 0:4] + stats[:, 4:8] + stats[:, 8:12])
    top = functools.reduce(jnp.maximum, logs)
    shares = [jnp.exp2(log - top) for log in logs]
    inverse = 1.0 / functools.reduce(jnp.add, shares)
    total = jnp.zeros((ROWS, COLS), jnp.float32)
    for part in range(count):
        share = shares[part] * inverse
        spread = jnp.zeros((ROWS, COLS), jnp.float32)
        for head in range(HEADS_HERE):
            inside = (lane >= head * HEAD) & (lane < (head + 1) * HEAD)
            spread = jnp.where(inside, share[:, head : head + 1], spread)
        total = total + spread * parts[part][:, :COLS].astype(jnp.float32)
    o_ref[...] = total.astype(jnp.bfloat16)


def combine(parts):
    return pl.pallas_call(
        combine_kernel,
        out_shape=jax.ShapeDtypeStruct((ROWS, COLS), jnp.bfloat16),
        compiler_params=pltpu.CompilerParams(vmem_limit_bytes=VMEM_LIMIT),
        name="combine",
    )(*parts)


def middle_kernel(
    place_ref, rows_ref, context_ref, w0, w1, w2, w3, gain_ref, glu_ref, m_ref, g_ref,
    weights, gain, glu, sems,
):
    copies = [
        pltpu.make_async_copy(weight, weights.at[index], sems.at[index])
        for index, weight in enumerate((w0, w1, w2, w3))
    ]
    copies.append(pltpu.make_async_copy(gain_ref, gain, sems.at[4]))
    for index in range(2):
        copies.append(pltpu.make_async_copy(glu_ref.at[index], glu.at[index], sems.at[5 + index]))
    for copy in copies:
        copy.start()
    place = place_ref[0]
    total = rows_ref[...].astype(jnp.float32)
    for offset in range(4):
        copies[offset].wait()
        total = total + jnp.dot(
            context_ref[place ^ offset], weights[offset], preferred_element_type=jnp.float32
        )
    middle = total.astype(jnp.bfloat16)
    for position in range(4):

        @pl.when(place == position)
        def _():
            m_ref[...] = middle[:, position * COLS : (position + 1) * COLS]

    copies[4].wait()
    normed = layer_norm(middle, gain[...].reshape(1, D))
    copies[5].wait()
    value = jnp.dot(normed, glu[0], preferred_element_type=jnp.float32)
    copies[6].wait()
    gate = jnp.dot(normed, glu[1], preferred_element_type=jnp.float32)
    g_ref[...] = (value * (1.0 / (1.0 + jnp.exp(-gate)))).astype(jnp.bfloat16)


def middle_and_glu(place, rows, context, weights, gain, glu_weight):
    count = rows.shape[0]
    vmem = pl.BlockSpec(memory_space=pltpu.VMEM)
    hbm = pl.BlockSpec(memory_space=pltpu.HBM)
    return pl.pallas_call(
        middle_kernel,
        in_specs=[pl.BlockSpec(memory_space=pltpu.SMEM), vmem, vmem] + [hbm] * 6,
        out_specs=[vmem] * 2,
        out_shape=[jax.ShapeDtypeStruct((count, COLS), jnp.bfloat16)] * 2,
        scratch_shapes=[
            pltpu.VMEM((4, COLS, D), jnp.bfloat16),
            pltpu.VMEM((D,), jnp.float32),
            pltpu.VMEM((2, D, COLS), jnp.bfloat16),
            pltpu.SemaphoreType.DMA((7,)),
        ],
        compiler_params=pltpu.CompilerParams(vmem_limit_bytes=VMEM_WHOLE),
        name="middle",
    )(place, rows, context, *weights, gain, glu_weight)


def depthwise_kernel(before_ref, glu_ref, after_ref, taps_ref, bias_ref, o_ref, held):
    held[:HALO] = before_ref[...].astype(jnp.float32)
    held[HALO : HALO + ROWS] = glu_ref[...].astype(jnp.float32)
    held[HALO + ROWS :] = after_ref[...].astype(jnp.float32)
    taps = taps_ref[...].astype(jnp.float32)
    for column in range(COLS // 128):
        here = slice(column * 128, (column + 1) * 128)
        total = jnp.zeros((ROWS, 128), jnp.float32) + bias_ref[here].reshape(1, 128)
        for tap in range(2 * REACH + 1):
            begin = HALO - REACH + tap
            total = total + held[begin : begin + ROWS, here] * taps[tap : tap + 1, here]
        o_ref[:, here] = (total / (1.0 + jnp.exp(-total))).astype(jnp.bfloat16)


def depthwise(before, glu, after, taps, bias):
    return pl.pallas_call(
        depthwise_kernel,
        out_shape=jax.ShapeDtypeStruct((ROWS, COLS), jnp.bfloat16),
        scratch_shapes=[pltpu.VMEM((ROWS + 2 * HALO, COLS), jnp.float32)],
        compiler_params=pltpu.CompilerParams(vmem_limit_bytes=VMEM_LIMIT),
        name="depthwise",
    )(before, glu, after, taps, bias)


def project_kernel(rows_ref, gain_ref, w_ref, kv_ref, q_ref, gain, weights, sems):
    copies = [pltpu.make_async_copy(gain_ref, gain, sems.at[3])]
    for index in (1, 2, 0):
        copies.append(pltpu.make_async_copy(w_ref.at[index], weights.at[index], sems.at[index]))
    for copy in copies:
        copy.start()
    rows = rows_ref[...].astype(jnp.float32)
    average = jnp.mean(rows, axis=-1, keepdims=True)
    centered = rows - average
    variance = jnp.mean(centered * centered, axis=-1, keepdims=True)
    scaled = centered * lax.rsqrt(variance + 1e-05)
    copies[0].wait()
    normed = (scaled * gain[...].reshape(1, D)).astype(jnp.bfloat16)
    for half in range(2):
        copies[1 + half].wait()
        kv_ref[:, half * COLS : (half + 1) * COLS] = jnp.dot(
            normed, weights[1 + half], preferred_element_type=jnp.float32
        ).astype(jnp.bfloat16)
    copies[3].wait()
    query = jnp.dot(normed, weights[0], preferred_element_type=jnp.float32)
    q_ref[...] = (query * Q_SCALE).astype(jnp.bfloat16)


def project(rows, gain, weights):
    vmem = pl.BlockSpec(memory_space=pltpu.VMEM)
    hbm = pl.BlockSpec(memory_space=pltpu.HBM)
    return pl.pallas_call(
        project_kernel,
        in_specs=[vmem, hbm, hbm],
        out_specs=[vmem, vmem],
        out_shape=[
            jax.ShapeDtypeStruct((ROWS, 2 * COLS), jnp.bfloat16),
            jax.ShapeDtypeStruct((ROWS, COLS), jnp.bfloat16),
        ],
        scratch_shapes=[
            pltpu.VMEM((D,), jnp.float32),
            pltpu.VMEM((3, D, COLS), jnp.bfloat16),
            pltpu.SemaphoreType.DMA((4,)),
        ],
        compiler_params=pltpu.CompilerParams(vmem_limit_bytes=VMEM_WHOLE),
        name="project",
    )(rows, gain, weights)


def part_kernel(place_ref, own_ref, other_ref, w_own, w_other, *refs):
    o_ref = refs[-1]
    columns = pl.ds(pl.multiple_of(place_ref[0] * COLS, 128), COLS)
    total = jnp.dot(own_ref[...], w_own[:, columns], preferred_element_type=jnp.float32)
    total = total + jnp.dot(
        other_ref[...], w_other[:, columns], preferred_element_type=jnp.float32
    )
    if len(refs) > 1:
        total = total + refs[0][...].astype(jnp.float32)
    o_ref[...] = total.astype(o_ref.dtype)


def part_sum(place, own, other, weights, extra, kind):
    vmem = pl.BlockSpec(memory_space=pltpu.VMEM)
    return pl.pallas_call(
        part_kernel,
        in_specs=[pl.BlockSpec(memory_space=pltpu.SMEM)] + [vmem] * (4 + len(extra)),
        out_specs=vmem,
        out_shape=jax.ShapeDtypeStruct((ROWS, COLS), kind),
        compiler_params=pltpu.CompilerParams(vmem_limit_bytes=VMEM_LIMIT),
        cost_estimate=pl.CostEstimate(
            flops=4 * ROWS * COLS * COLS, bytes_accessed=3 * 2**20, transcendentals=0
        ),
        name="part_sum",
    )(place, own, other, *weights, *extra)


def behind(values, *earlier):
    return lax.optimization_barrier((tuple(values),) + earlier)[0]


def swap(value, axis, count, flip):
    return lax.ppermute(value, axis, [(i, i ^ flip) for i in range(count)])


def shift(value, axis, count, offset):
    return lax.ppermute(value, axis, [(i, (i + offset) % count) for i in range(count)])


def per_device(
    frames,
    attn_gain,
    query_key_value,
    out_weight,
    conv_gain,
    glu_weight,
    depth_kernel,
    depth_bias,
    proj_weight,
):
    place = lax.axis_index(TP)
    out_core = swap(out_weight, "core", 2, 1)
    proj_core = swap(proj_weight, "core", 2, 1)
    whole_rows = lax.all_gather(frames, TP, axis=1, tiled=True)
    mine, query = project(whole_rows, attn_gain, query_key_value)
    lower1, upper1 = shift(mine, "z", 8, 1), shift(mine, "z", 8, -1)
    query1 = swap(query, "y", 4, 1)
    (out_here,) = behind((out_weight,), query1)
    out_far = swap(out_here, "xh", 2, 1)
    lower2, upper2 = shift(lower1, "z", 8, 1), shift(upper1, "z", 8, -1)
    pair2 = swap(jnp.concatenate([query, query1], 0), "y", 4, 2)
    half = ROWS // 2
    second = [
        shift(lower2, "z", 8, 1),
        shift(upper2, "z", 8, -1),
        shift(lower2[:half], "z", 8, 2),
        shift(upper2[half:], "z", 8, -2),
    ]
    blocks = [mine, lower1, upper1, lower2, upper2]
    prior2 = first_attention([pair2], blocks)
    prior0 = first_attention([query, query1], blocks)
    second = behind(second, prior0, prior2)
    partial2, partial3 = last_attention([pair2], second, prior2)
    part2, part3 = swap(partial2, "y", 4, 2), swap(partial3, "y", 4, 3)
    partial0, partial1 = last_attention([query, query1], second, prior0)
    part1 = swap(partial1, "y", 4, 1)
    (out_far_core,) = behind((out_far,), part2, part3, part1)
    out_far_core = swap(out_far_core, "core", 2, 1)
    out_pieces = (out_weight, out_core, out_far, out_far_core)
    parts = [partial0, part1, part2, part3]
    context = combine(parts)
    context = lax.all_gather(context, TP, axis=0, tiled=False)
    middle, glu = middle_and_glu(
        place.reshape(1), whole_rows, context, out_pieces, conv_gain, glu_weight
    )
    before = lax.ppermute(glu[ROWS - HALO :], CTX, [(i, i + 1) for i in range(31)])
    after = lax.ppermute(glu[:HALO], CTX, [(i + 1, i) for i in range(31)])
    activated = depthwise(before, glu, after, depth_kernel, depth_bias)
    other = swap(activated, "core", 2, 1)
    weights = (proj_weight, proj_core)
    theirs = part_sum((place ^ 2).reshape(1), activated, other, weights, (), jnp.bfloat16)
    theirs = swap(theirs, "xh", 2, 1)
    ours = part_sum(place.reshape(1), activated, other, weights, (middle,), jnp.float32)
    return (ours + theirs.astype(jnp.float32)).astype(jnp.bfloat16)


def solution(mesh):
    parted = Mesh(mesh.devices.reshape(2, 8, 4, 2, 2), ("batch", "z", "y", "xh", "core"))
    in_specs = (
        P(("batch",) + CTX, TP),
        P(),
        P(None, None, TP),
        P(TP, None),
        P(),
        P(None, None, TP),
        P(None, TP),
        P(TP),
        P(TP, None),
    )
    out_specs = P(("batch",) + CTX, TP)
    return jax.shard_map(
        per_device, mesh=parted, in_specs=in_specs, out_specs=out_specs, check_vma=False
    )
```

```python
import functools
import math

import jax
import jax.numpy as jnp
from jax import lax
from jax.experimental import pallas as pl
from jax.experimental.pallas import tpu as pltpu
from jax.sharding import Mesh
from jax.sharding import PartitionSpec as P

D = 1536
HEAD = 96
HEADS_HERE = 4
COLS = 384
ROWS = 192
REACH = 15
HALO = 16
STATS = 16
TP = ("xh", "core")
CTX = ("z", "y")
Q_SCALE = math.log2(math.e) / math.sqrt(HEAD)
VMEM_LIMIT = 8 * 2**20
OVERLAPPED = pl.CostEstimate(flops=2 * 10**10, bytes_accessed=2**20, transcendentals=0)


def layer_norm(inputs, gain):
    inputs = inputs.astype(jnp.float32)
    average = jnp.mean(inputs, axis=-1, keepdims=True)
    centered = inputs - average
    variance = jnp.mean(centered * centered, axis=-1, keepdims=True)
    return (centered * lax.rsqrt(variance + 1e-05) * gain).astype(jnp.bfloat16)


def split_three(value):
    high = value.astype(jnp.bfloat16).astype(jnp.float32)
    rest = value - high
    mid = rest.astype(jnp.bfloat16).astype(jnp.float32)
    return high, mid, rest - mid


def head_window(head):
    start = 0 if head < 2 else 128
    lane = lax.broadcasted_iota(jnp.int32, (1, 256), 1) + start
    return start, (lane >= head * HEAD) & (lane < (head + 1) * HEAD)


def attend(queries, keys, values, head):
    start, inside = head_window(head)
    masked = jnp.where(inside, queries[:, start : start + 256], 0)
    window = jnp.concatenate([block[:, start : start + 256] for block in keys], 0)
    scores = lax.dot_general(
        masked, window, (((1,), (1,)), ((), ())), preferred_element_type=jnp.float32
    )
    top = jnp.max(scores, axis=1, keepdims=True)
    weights = jnp.exp2(scores - top)
    denominator = jnp.sum(weights, axis=1, keepdims=True)
    window = jnp.concatenate([block[:, start : start + 256] for block in values], 0)
    summed = jnp.dot(weights.astype(jnp.bfloat16), window, preferred_element_type=jnp.float32)
    return inside, summed, top, denominator


def widen(part, head):
    blank = jnp.zeros((part.shape[0], 128), jnp.float32)
    return jnp.concatenate([part, blank] if head < 2 else [blank, part], 1)


def split_refs(refs, count):
    keys = [ref.at[:, :COLS] for ref in refs[:count]]
    values = [ref.at[:, COLS:] for ref in refs[:count]]
    return keys, values, refs[count:]


def first_attention_kernel(places, blocks, *refs):
    pieces, refs = refs[: len(places)], refs[len(places) :]
    keys, values, rest = split_refs(refs, blocks)
    o_ref, top_ref, sum_ref = rest
    lane = lax.broadcasted_iota(jnp.int32, (1, 128), 1)
    queries = [ref[at * ROWS : (at + 1) * ROWS] for ref, at in zip(pieces, places)]
    queries = jnp.concatenate(queries, 0)
    count = queries.shape[0]
    total = jnp.zeros((count, COLS), jnp.float32)
    tops = jnp.zeros((count, 128), jnp.float32)
    sums = jnp.ones((count, 128), jnp.float32)
    for head in range(HEADS_HERE):
        inside, summed, top, denominator = attend(queries, keys, values, head)
        total = total + widen(jnp.where(inside, summed, 0.0), head)
        tops = jnp.where(lane == head, top, tops)
        sums = jnp.where(lane == head, denominator, sums)
    o_ref[...] = total
    top_ref[...] = tops
    sum_ref[...] = sums


def last_attention_kernel(places, blocks, *refs):
    pieces, refs = refs[: len(places)], refs[len(places) :]
    keys, values, rest = split_refs(refs, blocks)
    prior_ref, top_ref, sum_ref, *outs = rest
    lane = lax.broadcasted_iota(jnp.int32, (1, 128), 1)
    queries = [ref[at * ROWS : (at + 1) * ROWS] for ref, at in zip(pieces, places)]
    queries = jnp.concatenate(queries, 0)
    count = queries.shape[0]
    tops = jnp.zeros((count, 128), jnp.float32)
    sums = jnp.zeros((count, 128), jnp.float32)
    products = []
    for head in range(HEADS_HERE):
        inside, summed, top, denominator = attend(queries, keys, values, head)
        products.append((inside, summed))
        tops = jnp.where(lane == head, top, tops)
        sums = jnp.where(lane == head, denominator, sums)
    joint = jnp.maximum(tops, top_ref[...])
    rescale = jnp.exp2(tops - joint)
    prior_rescale = jnp.exp2(top_ref[...] - joint)
    denominator = sums * rescale + sum_ref[...] * prior_rescale
    inverse = 1.0 / denominator
    rescale = rescale * inverse
    prior_rescale = prior_rescale * inverse
    total = jnp.zeros((count, COLS), jnp.float32)
    for head, (inside, summed) in enumerate(products):
        start = 0 if head < 2 else 128
        part = (
            summed * rescale[:, head : head + 1]
            + prior_ref[:, start : start + 256] * prior_rescale[:, head : head + 1]
        )
        total = total + widen(jnp.where(inside, part, 0.0), head)
    high, mid, low = split_three(joint + jnp.log2(denominator))
    stats = jnp.where(
        lane < 4, high, jnp.where(lane < 8, pltpu.roll(mid, 4, 1), pltpu.roll(low, 8, 1))
    )
    for place, out in enumerate(outs):
        rows = slice(place * ROWS, (place + 1) * ROWS)
        out[:ROWS] = total[rows].astype(jnp.bfloat16)
        turned = jnp.concatenate([stats[rows], jnp.zeros((256 - ROWS, 128), jnp.float32)], 0)
        turned = jnp.transpose(turned)[:STATS].astype(jnp.bfloat16)
        blank = jnp.zeros((STATS, COLS - 256), jnp.bfloat16)
        out[ROWS:] = jnp.concatenate([turned, blank], 1)


def attention_cost(rows, blocks):
    flops = 2 * 2 * rows * ROWS * blocks * 256 * HEADS_HERE
    return pl.CostEstimate(flops=flops, bytes_accessed=4 * 2**20, transcendentals=0)


def first_attention(queries, blocks):
    places = tuple(at for _, at in queries)
    rows = len(places) * ROWS
    return pl.pallas_call(
        functools.partial(first_attention_kernel, places, len(blocks)),
        out_shape=[
            jax.ShapeDtypeStruct((rows, COLS), jnp.float32),
            jax.ShapeDtypeStruct((rows, 128), jnp.float32),
            jax.ShapeDtypeStruct((rows, 128), jnp.float32),
        ],
        compiler_params=pltpu.CompilerParams(vmem_limit_bytes=VMEM_LIMIT),
        cost_estimate=attention_cost(rows, len(blocks)),
        name="first_attention",
    )(*[query for query, _ in queries], *blocks)


def last_attention(queries, blocks, prior):
    places = tuple(at for _, at in queries)
    rows = len(places) * ROWS
    return pl.pallas_call(
        functools.partial(last_attention_kernel, places, len(blocks)),
        out_shape=[jax.ShapeDtypeStruct((ROWS + STATS, COLS), jnp.bfloat16)] * (rows // ROWS),
        compiler_params=pltpu.CompilerParams(vmem_limit_bytes=VMEM_LIMIT),
        cost_estimate=attention_cost(rows, len(blocks)),
        name="last_attention",
    )(*[query for query, _ in queries], *blocks, *prior)


def combine_kernel(*refs):
    parts, o_ref = refs[:-1], refs[-1]
    lane = lax.broadcasted_iota(jnp.int32, (1, COLS), 1)
    logs = []
    for part in parts:
        stats = part[ROWS:, :256].astype(jnp.float32)
        logs.append(stats[0:4] + stats[4:8] + stats[8:12])
    top = functools.reduce(jnp.maximum, logs)
    shares = [jnp.exp2(log - top) for log in logs]
    inverse = 1.0 / functools.reduce(jnp.add, shares)
    shares = jnp.concatenate([share * inverse for share in shares], 0)
    blank = jnp.zeros((128 - shares.shape[0], 256), jnp.float32)
    shares = jnp.transpose(jnp.concatenate([shares, blank], 0))[:ROWS]
    total = jnp.zeros((ROWS, COLS), jnp.float32)
    for place, part in enumerate(parts):
        spread = jnp.zeros((ROWS, COLS), jnp.float32)
        for head in range(HEADS_HERE):
            inside = (lane >= head * HEAD) & (lane < (head + 1) * HEAD)
            column = place * HEADS_HERE + head
            spread = jnp.where(inside, shares[:, column : column + 1], spread)
        total = total + spread * part[:ROWS].astype(jnp.float32)
    o_ref[...] = total.astype(jnp.bfloat16)


def combine(parts):
    return pl.pallas_call(
        combine_kernel,
        out_shape=jax.ShapeDtypeStruct((ROWS, COLS), jnp.bfloat16),
        compiler_params=pltpu.CompilerParams(vmem_limit_bytes=VMEM_LIMIT),
        cost_estimate=OVERLAPPED,
        name="combine",
    )(*parts)


def middle_kernel(
    rows_ref, context_ref, w0, w1, w2, w3, gain_ref, glu_ref, m_ref, g_ref, top_ref, end_ref
):
    place = lax.axis_index(TP)
    total = rows_ref[...].astype(jnp.float32)
    for offset, weight in enumerate((w0, w1, w2, w3)):
        total = total + jnp.dot(
            context_ref[place ^ offset], weight[...], preferred_element_type=jnp.float32
        )
    middle = total.astype(jnp.bfloat16)
    for position in range(4):

        @pl.when(place == position)
        def _():
            m_ref[...] = middle[:, position * COLS : (position + 1) * COLS]

    normed = layer_norm(middle, gain_ref[...].reshape(1, D))
    value = jnp.dot(normed, glu_ref[0], preferred_element_type=jnp.float32)
    gate = jnp.dot(normed, glu_ref[1], preferred_element_type=jnp.float32)
    glu = (value * (1.0 / (1.0 + jnp.exp(-gate)))).astype(jnp.bfloat16)
    g_ref[...] = glu
    top_ref[...] = glu[:HALO]
    end_ref[...] = glu[ROWS - HALO :]


def middle_and_glu(rows, context, weights, gain, glu_weight):
    vmem = pl.BlockSpec(memory_space=pltpu.VMEM)
    return pl.pallas_call(
        middle_kernel,
        in_specs=[vmem] * 8,
        out_specs=[vmem] * 4,
        out_shape=[jax.ShapeDtypeStruct((ROWS, COLS), jnp.bfloat16)] * 2
        + [jax.ShapeDtypeStruct((HALO, COLS), jnp.bfloat16)] * 2,
        compiler_params=pltpu.CompilerParams(vmem_limit_bytes=VMEM_LIMIT),
        cost_estimate=OVERLAPPED,
        name="middle",
    )(rows, context, *weights, gain, glu_weight)


def convolve(held, taps_ref, bias_ref, count, store):
    taps = taps_ref[...].astype(jnp.float32)
    for column in range(COLS // 128):
        here = slice(column * 128, (column + 1) * 128)
        total = jnp.zeros((count, 128), jnp.float32) + bias_ref[here].reshape(1, 128)
        for tap in range(2 * REACH + 1):
            begin = HALO - REACH + tap
            total = total + held[begin : begin + count, here] * taps[tap : tap + 1, here]
        store(here, (total / (1.0 + jnp.exp(-total))).astype(jnp.bfloat16))


def inner_kernel(glu_ref, taps_ref, bias_ref, o_ref, held):
    held[...] = glu_ref[...].astype(jnp.float32)

    def store(here, value):
        o_ref[:, here] = value

    convolve(held, taps_ref, bias_ref, ROWS - 2 * HALO, store)


def edges_kernel(before_ref, glu_ref, after_ref, inner_ref, taps_ref, bias_ref, o_ref, held):
    o_ref[HALO : ROWS - HALO] = inner_ref[...]
    for side in range(2):
        if side == 0:
            held[:HALO] = before_ref[...].astype(jnp.float32)
            held[HALO:] = glu_ref[: 2 * HALO].astype(jnp.float32)
        else:
            held[: 2 * HALO] = glu_ref[ROWS - 2 * HALO :].astype(jnp.float32)
            held[2 * HALO :] = after_ref[...].astype(jnp.float32)

        def store(here, value):
            o_ref[side * (ROWS - HALO) : side * (ROWS - HALO) + HALO, here] = value

        convolve(held, taps_ref, bias_ref, HALO, store)


def depthwise(before, glu, after, taps, bias):
    inner = pl.pallas_call(
        inner_kernel,
        out_shape=jax.ShapeDtypeStruct((ROWS - 2 * HALO, COLS), jnp.bfloat16),
        scratch_shapes=[pltpu.VMEM((ROWS, COLS), jnp.float32)],
        compiler_params=pltpu.CompilerParams(vmem_limit_bytes=VMEM_LIMIT),
        name="inner",
    )(glu, taps, bias)
    return pl.pallas_call(
        edges_kernel,
        out_shape=jax.ShapeDtypeStruct((ROWS, COLS), jnp.bfloat16),
        scratch_shapes=[pltpu.VMEM((3 * HALO, COLS), jnp.float32)],
        compiler_params=pltpu.CompilerParams(vmem_limit_bytes=VMEM_LIMIT),
        name="edges",
    )(before, glu, after, inner, taps, bias)


def project_kernel(rows_ref, gain_ref, w_ref, kv_ref, q_ref):
    normed = layer_norm(rows_ref[...], gain_ref[...].reshape(1, D))
    for half in range(2):
        kv_ref[:, half * COLS : (half + 1) * COLS] = jnp.dot(
            normed, w_ref[1 + half], preferred_element_type=jnp.float32
        ).astype(jnp.bfloat16)
    query = jnp.dot(normed, w_ref[0], preferred_element_type=jnp.float32)
    q_ref[...] = (query * Q_SCALE).astype(jnp.bfloat16)


def project(rows, gain, weights):
    return pl.pallas_call(
        project_kernel,
        out_shape=[
            jax.ShapeDtypeStruct((ROWS, 2 * COLS), jnp.bfloat16),
            jax.ShapeDtypeStruct((ROWS, COLS), jnp.bfloat16),
        ],
        compiler_params=pltpu.CompilerParams(vmem_limit_bytes=VMEM_LIMIT),
        name="project",
    )(rows, gain, weights)


def stage_kernel(frames_ref, o_ref):
    o_ref[...] = frames_ref[...]


def stage(frames):
    return pl.pallas_call(
        stage_kernel,
        out_shape=jax.ShapeDtypeStruct(frames.shape, frames.dtype),
        compiler_params=pltpu.CompilerParams(vmem_limit_bytes=VMEM_LIMIT),
        cost_estimate=OVERLAPPED,
        name="stage",
    )(frames)


def join_kernel(a_ref, b_ref, o_ref):
    o_ref[:ROWS] = a_ref[...]
    o_ref[ROWS:] = b_ref[...]


def join(a, b):
    return pl.pallas_call(
        join_kernel,
        out_shape=jax.ShapeDtypeStruct((2 * ROWS, COLS), jnp.bfloat16),
        compiler_params=pltpu.CompilerParams(vmem_limit_bytes=VMEM_LIMIT),
        name="join",
    )(a, b)


def halves_kernel(a_ref, b_ref, a_out, b_out):
    a_out[...] = a_ref[: ROWS // 2]
    b_out[...] = b_ref[ROWS // 2 :]


def halves(a, b):
    return pl.pallas_call(
        halves_kernel,
        out_shape=[jax.ShapeDtypeStruct((ROWS // 2, 2 * COLS), jnp.bfloat16)] * 2,
        compiler_params=pltpu.CompilerParams(vmem_limit_bytes=VMEM_LIMIT),
        name="halves",
    )(a, b)


def part_kernel(flip, own_ref, other_ref, w_own, w_other, *refs):
    o_ref = refs[-1]
    columns = pl.ds(pl.multiple_of((lax.axis_index(TP) ^ flip) * COLS, 128), COLS)
    total = jnp.dot(own_ref[...], w_own[:, columns], preferred_element_type=jnp.float32)
    total = total + jnp.dot(
        other_ref[...], w_other[:, columns], preferred_element_type=jnp.float32
    )
    for extra in refs[:-1]:
        total = total + extra[...].astype(jnp.float32)
    o_ref[...] = total.astype(o_ref.dtype)


def part_sum(flip, own, other, weights, extra):
    vmem = pl.BlockSpec(memory_space=pltpu.VMEM)
    return pl.pallas_call(
        functools.partial(part_kernel, flip),
        in_specs=[vmem] * (4 + len(extra)),
        out_specs=vmem,
        out_shape=jax.ShapeDtypeStruct((ROWS, COLS), jnp.bfloat16),
        compiler_params=pltpu.CompilerParams(vmem_limit_bytes=VMEM_LIMIT),
        cost_estimate=pl.CostEstimate(
            flops=4 * ROWS * COLS * COLS, bytes_accessed=3 * 2**20, transcendentals=0
        ),
        name="part_sum",
    )(own, other, *weights, *extra)


def swap(value, axis, count, flip):
    return lax.ppermute(value, axis, [(i, i ^ flip) for i in range(count)])


def shift(value, axis, count, offset):
    return lax.ppermute(value, axis, [(i, (i + offset) % count) for i in range(count)])


def per_device(
    frames,
    attn_gain,
    query_key_value,
    out_weight,
    conv_gain,
    glu_weight,
    depth_kernel,
    depth_bias,
    proj_weight,
):
    out_core = swap(out_weight, "core", 2, 1)
    out_far = swap(out_weight, "xh", 2, 1)
    whole_rows = lax.all_gather(stage(frames), TP, axis=1, tiled=True)
    mine, query = project(whole_rows, attn_gain, query_key_value)
    lower1, upper1 = shift(mine, "z", 8, 1), shift(mine, "z", 8, -1)
    query1 = swap(query, "y", 4, 1)
    lower2, upper2 = shift(lower1, "z", 8, 1), shift(upper1, "z", 8, -1)
    pair2 = swap(join(query, query1), "y", 4, 2)
    low_half, high_half = halves(lower2, upper2)
    second = [
        shift(lower2, "z", 8, 1),
        shift(upper2, "z", 8, -1),
        shift(low_half, "z", 8, 2),
        shift(high_half, "z", 8, -2),
    ]
    blocks = [mine, lower1, upper1, lower2, upper2]
    groups = ([(pair2, 0)], [(query1, 0), (pair2, 1)], [(query, 0)])
    priors = [first_attention(group, blocks) for group in groups]
    (partial2,) = last_attention(groups[0], second, priors[0])
    part2 = swap(partial2, "y", 4, 2)
    partial1, partial3 = last_attention(groups[1], second, priors[1])
    part1, part3 = swap(partial1, "y", 4, 1), swap(partial3, "y", 4, 3)
    (partial0,) = last_attention(groups[2], second, priors[2])
    out_far_core = swap(out_far, "core", 2, 1)
    out_pieces = (out_weight, out_core, out_far, out_far_core)
    context = combine([partial0, part1, part2, part3])
    proj_core = swap(proj_weight, "core", 2, 1)
    context = lax.all_gather(context, TP, axis=0, tiled=False)
    middle, glu, top, end = middle_and_glu(
        whole_rows, context, out_pieces, conv_gain, glu_weight
    )
    before = lax.ppermute(end, CTX, [(i, i + 1) for i in range(31)])
    after = lax.ppermute(top, CTX, [(i + 1, i) for i in range(31)])
    activated = depthwise(before, glu, after, depth_kernel, depth_bias)
    other = swap(activated, "core", 2, 1)
    weights = (proj_weight, proj_core)
    theirs = swap(part_sum(2, activated, other, weights, ()), "xh", 2, 1)
    return part_sum(0, activated, other, weights, (middle, theirs))


def solution(mesh):
    parted = Mesh(mesh.devices.reshape(2, 8, 4, 2, 2), ("batch", "z", "y", "xh", "core"))
    in_specs = (
        P(("batch",) + CTX, TP),
        P(),
        P(None, None, TP),
        P(TP, None),
        P(),
        P(None, None, TP),
        P(None, TP),
        P(TP),
        P(TP, None),
    )
    out_specs = P(("batch",) + CTX, TP)
    return jax.shard_map(
        per_device, mesh=parted, in_specs=in_specs, out_specs=out_specs, check_vma=False
    )
```

```python
import functools
import math

import jax
import jax.numpy as jnp
from jax import lax
from jax.experimental import pallas as pl
from jax.experimental.pallas import tpu as pltpu
from jax.sharding import Mesh
from jax.sharding import PartitionSpec as P

D = 1536
HEAD = 96
HEADS_HERE = 4
COLS = 384
ROWS = 192
REACH = 15
HALO = 16
INNER = ROWS - 2 * HALO
STATS = 16
TP = ("xh", "core")
CTX = ("z", "y")
Q_SCALE = math.log2(math.e) / math.sqrt(HEAD)
VMEM_LIMIT = 8 * 2**20
OVERLAPPED = pl.CostEstimate(flops=2 * 10**10, bytes_accessed=2**20, transcendentals=0)


def layer_norm(inputs, gain, eps=1e-05):
    inputs = inputs.astype(jnp.float32)
    average = jnp.mean(inputs, axis=-1, keepdims=True)
    centered = inputs - average
    variance = jnp.mean(centered * centered, axis=-1, keepdims=True)
    return (centered * lax.rsqrt(variance + eps) * gain).astype(jnp.bfloat16)


def split_three(value):
    high = value.astype(jnp.bfloat16).astype(jnp.float32)
    rest = value - high
    mid = rest.astype(jnp.bfloat16).astype(jnp.float32)
    return high, mid, rest - mid


def head_mask(head):
    start = 128 * (head // 2)
    lane = lax.broadcasted_iota(jnp.int32, (1, 256), 1) + start
    return (lane >= head * HEAD) & (lane < (head + 1) * HEAD)


def attend(queries, keys, values, pair):
    start = 128 * pair
    window = queries[:, start : start + 256]
    masks = [head_mask(2 * pair + side) for side in range(2)]
    masked = jnp.concatenate([jnp.where(mask, window, 0) for mask in masks], 0)
    window = jnp.concatenate([block[:, start : start + 256] for block in keys], 0)
    scores = lax.dot_general(
        masked, window, (((1,), (1,)), ((), ())), preferred_element_type=jnp.float32
    )
    top = jnp.max(scores, axis=1, keepdims=True)
    weights = jnp.exp2(scores - top)
    denominator = jnp.sum(weights, axis=1, keepdims=True)
    window = jnp.concatenate([block[:, start : start + 256] for block in values], 0)
    summed = jnp.dot(weights.astype(jnp.bfloat16), window, preferred_element_type=jnp.float32)
    return masks, summed, top, denominator


def widen(part, pair):
    blank = jnp.zeros((part.shape[0], 128), jnp.float32)
    return jnp.concatenate([part, blank] if pair == 0 else [blank, part], 1)


def split_refs(refs, count):
    keys = [ref.at[:, :COLS] for ref in refs[:count]]
    values = [ref.at[:, COLS:] for ref in refs[:count]]
    return keys, values, refs[count:]


def first_attention_kernel(places, blocks, *refs):
    pieces, refs = refs[: len(places)], refs[len(places) :]
    keys, values, rest = split_refs(refs, blocks)
    o_ref, top_ref, sum_ref = rest
    lane = lax.broadcasted_iota(jnp.int32, (1, 128), 1)
    queries = [ref[at * ROWS : (at + 1) * ROWS] for ref, at in zip(pieces, places)]
    queries = jnp.concatenate(queries, 0)
    count = queries.shape[0]
    total = jnp.zeros((count, COLS), jnp.float32)
    tops = jnp.zeros((count, 128), jnp.float32)
    sums = jnp.ones((count, 128), jnp.float32)
    for pair in range(2):
        masks, summed, top, denominator = attend(queries, keys, values, pair)
        both = jnp.where(masks[0], summed[:count], jnp.where(masks[1], summed[count:], 0.0))
        total = total + widen(both, pair)
        for side in range(2):
            rows = slice(side * count, (side + 1) * count)
            tops = jnp.where(lane == 2 * pair + side, top[rows], tops)
            sums = jnp.where(lane == 2 * pair + side, denominator[rows], sums)
    o_ref[...] = total
    top_ref[...] = tops
    sum_ref[...] = sums


def last_attention_kernel(places, blocks, *refs):
    pieces, refs = refs[: len(places)], refs[len(places) :]
    keys, values, rest = split_refs(refs, blocks)
    prior_ref, top_ref, sum_ref, *outs = rest
    lane = lax.broadcasted_iota(jnp.int32, (1, 128), 1)
    queries = [ref[at * ROWS : (at + 1) * ROWS] for ref, at in zip(pieces, places)]
    queries = jnp.concatenate(queries, 0)
    count = queries.shape[0]
    tops = jnp.zeros((count, 128), jnp.float32)
    sums = jnp.zeros((count, 128), jnp.float32)
    products = []
    for pair in range(2):
        masks, summed, top, denominator = attend(queries, keys, values, pair)
        products.append((masks, summed))
        for side in range(2):
            rows = slice(side * count, (side + 1) * count)
            tops = jnp.where(lane == 2 * pair + side, top[rows], tops)
            sums = jnp.where(lane == 2 * pair + side, denominator[rows], sums)
    joint = jnp.maximum(tops, top_ref[...])
    rescale = jnp.exp2(tops - joint)
    prior_rescale = jnp.exp2(top_ref[...] - joint)
    denominator = sums * rescale + sum_ref[...] * prior_rescale
    inverse = 1.0 / denominator
    rescale = rescale * inverse
    prior_rescale = prior_rescale * inverse
    total = jnp.zeros((count, COLS), jnp.float32)
    for pair, (masks, summed) in enumerate(products):
        prior = prior_ref[:, 128 * pair : 128 * pair + 256]
        both = jnp.zeros((count, 256), jnp.float32)
        for side, mask in enumerate(masks):
            head = slice(2 * pair + side, 2 * pair + side + 1)
            part = summed[side * count : (side + 1) * count] * rescale[:, head]
            both = jnp.where(mask, part + prior * prior_rescale[:, head], both)
        total = total + widen(both, pair)
    high, mid, low = split_three(joint + jnp.log2(denominator))
    stats = jnp.where(
        lane < 4, high, jnp.where(lane < 8, pltpu.roll(mid, 4, 1), pltpu.roll(low, 8, 1))
    )
    for place, out in enumerate(outs):
        rows = slice(place * ROWS, (place + 1) * ROWS)
        out[:ROWS] = total[rows].astype(jnp.bfloat16)
        turned = jnp.concatenate([stats[rows], jnp.zeros((256 - ROWS, 128), jnp.float32)], 0)
        turned = jnp.transpose(turned)[:STATS].astype(jnp.bfloat16)
        blank = jnp.zeros((STATS, COLS - 256), jnp.bfloat16)
        out[ROWS:] = jnp.concatenate([turned, blank], 1)


def attention_cost(rows, blocks):
    flops = 2 * 2 * rows * ROWS * blocks * 256 * HEADS_HERE
    return pl.CostEstimate(flops=flops, bytes_accessed=4 * 2**20, transcendentals=0)


def first_attention(queries, blocks):
    places = tuple(at for _, at in queries)
    rows = len(places) * ROWS
    return pl.pallas_call(
        functools.partial(first_attention_kernel, places, len(blocks)),
        out_shape=[
            jax.ShapeDtypeStruct((rows, COLS), jnp.float32),
            jax.ShapeDtypeStruct((rows, 128), jnp.float32),
            jax.ShapeDtypeStruct((rows, 128), jnp.float32),
        ],
        compiler_params=pltpu.CompilerParams(vmem_limit_bytes=VMEM_LIMIT),
        cost_estimate=attention_cost(rows, len(blocks)),
        name="first_attention",
    )(*[query for query, _ in queries], *blocks)


def last_attention(queries, blocks, prior):
    places = tuple(at for _, at in queries)
    rows = len(places) * ROWS
    return pl.pallas_call(
        functools.partial(last_attention_kernel, places, len(blocks)),
        out_shape=[jax.ShapeDtypeStruct((ROWS + STATS, COLS), jnp.bfloat16)] * (rows // ROWS),
        compiler_params=pltpu.CompilerParams(vmem_limit_bytes=VMEM_LIMIT),
        cost_estimate=attention_cost(rows, len(blocks)),
        name="last_attention",
    )(*[query for query, _ in queries], *blocks, *prior)


def combine_kernel(*refs):
    parts, o_ref = refs[:-1], refs[-1]
    lane = lax.broadcasted_iota(jnp.int32, (1, COLS), 1)
    logs = []
    for part in parts:
        stats = part[ROWS:, :256].astype(jnp.float32)
        logs.append(stats[0:4] + stats[4:8] + stats[8:12])
    top = functools.reduce(jnp.maximum, logs)
    shares = [jnp.exp2(log - top) for log in logs]
    inverse = 1.0 / functools.reduce(jnp.add, shares)
    shares = jnp.concatenate([share * inverse for share in shares], 0)
    blank = jnp.zeros((128 - shares.shape[0], 256), jnp.float32)
    shares = jnp.transpose(jnp.concatenate([shares, blank], 0))[:ROWS]
    total = jnp.zeros((ROWS, COLS), jnp.float32)
    for place, part in enumerate(parts):
        spread = jnp.zeros((ROWS, COLS), jnp.float32)
        for head in range(HEADS_HERE):
            inside = (lane >= head * HEAD) & (lane < (head + 1) * HEAD)
            column = place * HEADS_HERE + head
            spread = jnp.where(inside, shares[:, column : column + 1], spread)
        total = total + spread * part[:ROWS].astype(jnp.float32)
    o_ref[...] = total.astype(jnp.bfloat16)


def combine(parts):
    return pl.pallas_call(
        combine_kernel,
        out_shape=jax.ShapeDtypeStruct((ROWS, COLS), jnp.bfloat16),
        compiler_params=pltpu.CompilerParams(vmem_limit_bytes=VMEM_LIMIT),
        cost_estimate=OVERLAPPED,
        name="combine",
    )(*parts)


def middle_kernel(
    rows_ref, context_ref, w0, w1, w2, w3, gain_ref, glu_ref, m_ref, g_ref, top_ref, end_ref
):
    place = lax.axis_index(TP)
    total = rows_ref[...].astype(jnp.float32)
    for offset, weight in enumerate((w0, w1, w2, w3)):
        total = total + jnp.dot(
            context_ref[place ^ offset], weight[...], preferred_element_type=jnp.float32
        )
    middle = total.astype(jnp.bfloat16)
    for position in range(4):

        @pl.when(place == position)
        def _():
            m_ref[...] = middle[:, position * COLS : (position + 1) * COLS]

    normed = layer_norm(middle, gain_ref[...].reshape(1, D))
    value = jnp.dot(normed, glu_ref[0], preferred_element_type=jnp.float32)
    gate = jnp.dot(normed, glu_ref[1], preferred_element_type=jnp.float32)
    glu = (value * (1.0 / (1.0 + jnp.exp(-gate)))).astype(jnp.bfloat16)
    g_ref[...] = glu
    top_ref[...] = glu[:HALO]
    end_ref[...] = glu[ROWS - HALO :]


def middle_and_glu(rows, context, weights, gain, glu_weight):
    vmem = pl.BlockSpec(memory_space=pltpu.VMEM)
    return pl.pallas_call(
        middle_kernel,
        in_specs=[vmem] * 8,
        out_specs=[vmem] * 4,
        out_shape=[jax.ShapeDtypeStruct((ROWS, COLS), jnp.bfloat16)] * 2
        + [jax.ShapeDtypeStruct((HALO, COLS), jnp.bfloat16)] * 2,
        compiler_params=pltpu.CompilerParams(vmem_limit_bytes=VMEM_LIMIT),
        cost_estimate=OVERLAPPED,
        name="middle",
    )(rows, context, *weights, gain, glu_weight)


def convolve(held, taps_ref, bias_ref, count, store):
    taps = taps_ref[...].astype(jnp.float32)
    for column in range(COLS // 128):
        here = slice(column * 128, (column + 1) * 128)
        total = jnp.zeros((count, 128), jnp.float32) + bias_ref[here].reshape(1, 128)
        for tap in range(2 * REACH + 1):
            begin = HALO - REACH + tap
            total = total + held[begin : begin + count, here] * taps[tap : tap + 1, here]
        store(here, (total / (1.0 + jnp.exp(-total))).astype(jnp.bfloat16))


def inner_kernel(glu_ref, taps_ref, bias_ref, o_ref, held):
    held[...] = glu_ref[...].astype(jnp.float32)

    def store(here, value):
        o_ref[:, here] = value

    convolve(held, taps_ref, bias_ref, ROWS - 2 * HALO, store)


def edges_kernel(before_ref, glu_ref, after_ref, taps_ref, bias_ref, o_ref, held):
    for side in range(2):
        if side == 0:
            held[:HALO] = before_ref[...].astype(jnp.float32)
            held[HALO:] = glu_ref[: 2 * HALO].astype(jnp.float32)
        else:
            held[: 2 * HALO] = glu_ref[ROWS - 2 * HALO :].astype(jnp.float32)
            held[2 * HALO :] = after_ref[...].astype(jnp.float32)

        def store(here, value):
            o_ref[side * HALO : (side + 1) * HALO, here] = value

        convolve(held, taps_ref, bias_ref, HALO, store)


def conv_inner(glu, taps, bias):
    return pl.pallas_call(
        inner_kernel,
        out_shape=jax.ShapeDtypeStruct((INNER, COLS), jnp.bfloat16),
        scratch_shapes=[pltpu.VMEM((ROWS, COLS), jnp.float32)],
        compiler_params=pltpu.CompilerParams(vmem_limit_bytes=VMEM_LIMIT),
        name="inner",
    )(glu, taps, bias)


def conv_edges(before, glu, after, taps, bias):
    return pl.pallas_call(
        edges_kernel,
        out_shape=jax.ShapeDtypeStruct((2 * HALO, COLS), jnp.bfloat16),
        scratch_shapes=[pltpu.VMEM((3 * HALO, COLS), jnp.float32)],
        compiler_params=pltpu.CompilerParams(vmem_limit_bytes=VMEM_LIMIT),
        cost_estimate=OVERLAPPED,
        name="edges",
    )(before, glu, after, taps, bias)


def project_kernel(eps_ref, rows_ref, gain_ref, w_ref, kv_ref, q_ref):
    normed = layer_norm(rows_ref[...], gain_ref[...].reshape(1, D), eps_ref[0:1, 0:1])
    for half in range(2):
        kv_ref[:, half * COLS : (half + 1) * COLS] = jnp.dot(
            normed, w_ref[1 + half], preferred_element_type=jnp.float32
        ).astype(jnp.bfloat16)
    query = jnp.dot(normed, w_ref[0], preferred_element_type=jnp.float32)
    q_ref[...] = (query * Q_SCALE).astype(jnp.bfloat16)


def project(eps, rows, gain, weights):
    return pl.pallas_call(
        project_kernel,
        out_shape=[
            jax.ShapeDtypeStruct((ROWS, 2 * COLS), jnp.bfloat16),
            jax.ShapeDtypeStruct((ROWS, COLS), jnp.bfloat16),
        ],
        compiler_params=pltpu.CompilerParams(vmem_limit_bytes=VMEM_LIMIT),
        name="project",
    )(eps, rows, gain, weights)


def epsilon_kernel(o_ref):
    o_ref[...] = jnp.full((8, 128), 1e-05, jnp.float32)


def epsilon():
    return pl.pallas_call(
        epsilon_kernel,
        out_shape=jax.ShapeDtypeStruct((8, 128), jnp.float32),
        compiler_params=pltpu.CompilerParams(vmem_limit_bytes=VMEM_LIMIT),
        cost_estimate=OVERLAPPED,
        name="epsilon",
    )()


def join_kernel(a_ref, b_ref, o_ref):
    o_ref[:ROWS] = a_ref[...]
    o_ref[ROWS:] = b_ref[...]


def join(a, b):
    return pl.pallas_call(
        join_kernel,
        out_shape=jax.ShapeDtypeStruct((2 * ROWS, COLS), jnp.bfloat16),
        compiler_params=pltpu.CompilerParams(vmem_limit_bytes=VMEM_LIMIT),
        name="join",
    )(a, b)


def halves_kernel(a_ref, b_ref, a_out, b_out):
    a_out[...] = a_ref[: ROWS // 2]
    b_out[...] = b_ref[ROWS // 2 :]


def halves(a, b):
    return pl.pallas_call(
        halves_kernel,
        out_shape=[jax.ShapeDtypeStruct((ROWS // 2, 2 * COLS), jnp.bfloat16)] * 2,
        compiler_params=pltpu.CompilerParams(vmem_limit_bytes=VMEM_LIMIT),
        name="halves",
    )(a, b)


def product(flip, own_ref, other_ref, w_own, w_other):
    columns = pl.ds(pl.multiple_of((lax.axis_index(TP) ^ flip) * COLS, 128), COLS)
    total = jnp.dot(own_ref[...], w_own[:, columns], preferred_element_type=jnp.float32)
    return total + jnp.dot(
        other_ref[...], w_other[:, columns], preferred_element_type=jnp.float32
    )


def part_kernel(flip, own_ref, other_ref, w_own, w_other, o_ref):
    o_ref[...] = product(flip, own_ref, other_ref, w_own, w_other).astype(o_ref.dtype)


def part_sum(flip, own, other, weights, kind):
    return pl.pallas_call(
        functools.partial(part_kernel, flip),
        out_shape=jax.ShapeDtypeStruct(own.shape, kind),
        compiler_params=pltpu.CompilerParams(vmem_limit_bytes=VMEM_LIMIT),
        name="part_sum",
    )(own, other, *weights)


def final_kernel(own_ref, other_ref, w_own, w_other, middle_ref, ours_ref, inner_ref, edges_ref, o_ref):
    here = slice(HALO, HALO + INNER)
    total = ours_ref[...] + inner_ref[...].astype(jnp.float32)
    o_ref[here] = (middle_ref[here].astype(jnp.float32) + total).astype(jnp.bfloat16)
    total = product(0, own_ref, other_ref, w_own, w_other) + edges_ref[...].astype(jnp.float32)
    for side in range(2):
        here = slice(side * (ROWS - HALO), side * (ROWS - HALO) + HALO)
        part = total[side * HALO : (side + 1) * HALO]
        o_ref[here] = (middle_ref[here].astype(jnp.float32) + part).astype(jnp.bfloat16)


def final(own, other, weights, middle, ours, inner, edges):
    return pl.pallas_call(
        final_kernel,
        out_shape=jax.ShapeDtypeStruct((ROWS, COLS), jnp.bfloat16),
        compiler_params=pltpu.CompilerParams(vmem_limit_bytes=VMEM_LIMIT),
        name="final",
    )(own, other, *weights, middle, ours, inner, edges)


def swap(value, axis, count, flip):
    return lax.ppermute(value, axis, [(i, i ^ flip) for i in range(count)])


def shift(value, axis, count, offset):
    return lax.ppermute(value, axis, [(i, (i + offset) % count) for i in range(count)])


def per_device(
    frames,
    attn_gain,
    query_key_value,
    out_weight,
    conv_gain,
    glu_weight,
    depth_kernel,
    depth_bias,
    proj_weight,
):
    out_core = swap(out_weight, "core", 2, 1)
    out_far = swap(out_weight, "xh", 2, 1)
    whole_rows = lax.all_gather(frames, TP, axis=1, tiled=True)
    mine, query = project(epsilon(), whole_rows, attn_gain, query_key_value)
    lower1, upper1 = shift(mine, "z", 8, 1), shift(mine, "z", 8, -1)
    query1 = swap(query, "y", 4, 1)
    lower2, upper2 = shift(lower1, "z", 8, 1), shift(upper1, "z", 8, -1)
    pair2 = swap(join(query, query1), "y", 4, 2)
    low_half, high_half = halves(lower2, upper2)
    second = [
        shift(lower2, "z", 8, 1),
        shift(upper2, "z", 8, -1),
        shift(low_half, "z", 8, 2),
        shift(high_half, "z", 8, -2),
    ]
    blocks = [mine, lower1, upper1, lower2, upper2]
    groups = ([(pair2, 0)], [(query1, 0), (pair2, 1)], [(query, 0)])
    priors = [first_attention(group, blocks) for group in groups]
    (partial2,) = last_attention(groups[0], second, priors[0])
    part2 = swap(partial2, "y", 4, 2)
    partial1, partial3 = last_attention(groups[1], second, priors[1])
    part1, part3 = swap(partial1, "y", 4, 1), swap(partial3, "y", 4, 3)
    (partial0,) = last_attention(groups[2], second, priors[2])
    out_far_core = swap(out_far, "core", 2, 1)
    out_pieces = (out_weight, out_core, out_far, out_far_core)
    context = combine([partial0, part1, part2, part3])
    proj_core = swap(proj_weight, "core", 2, 1)
    context = lax.all_gather(context, TP, axis=0, tiled=False)
    middle, glu, top, end = middle_and_glu(
        whole_rows, context, out_pieces, conv_gain, glu_weight
    )
    before = lax.ppermute(end, CTX, [(i, i + 1) for i in range(31)])
    after = lax.ppermute(top, CTX, [(i + 1, i) for i in range(31)])
    weights = (proj_weight, proj_core)
    inner = conv_inner(glu, depth_kernel, depth_bias)
    inner_other = swap(inner, "core", 2, 1)
    inner_far = swap(part_sum(2, inner, inner_other, weights, jnp.bfloat16), "xh", 2, 1)
    ours = part_sum(0, inner, inner_other, weights, jnp.float32)
    edges = conv_edges(before, glu, after, depth_kernel, depth_bias)
    edges_other = swap(edges, "core", 2, 1)
    edges_far = swap(part_sum(2, edges, edges_other, weights, jnp.bfloat16), "xh", 2, 1)
    return final(edges, edges_other, weights, middle, ours, inner_far, edges_far)


def solution(mesh):
    parted = Mesh(mesh.devices.reshape(2, 8, 4, 2, 2), ("batch", "z", "y", "xh", "core"))
    in_specs = (
        P(("batch",) + CTX, TP),
        P(),
        P(None, None, TP),
        P(TP, None),
        P(),
        P(None, None, TP),
        P(None, TP),
        P(TP),
        P(TP, None),
    )
    out_specs = P(("batch",) + CTX, TP)
    return jax.shard_map(
        per_device, mesh=parted, in_specs=in_specs, out_specs=out_specs, check_vma=False
    )
```

```python
import functools
import math

import jax
import jax.numpy as jnp
from jax import lax
from jax.experimental import pallas as pl
from jax.experimental.pallas import tpu as pltpu
from jax.sharding import Mesh
from jax.sharding import PartitionSpec as P

D = 1536
HEAD = 96
HEADS_HERE = 4
COLS = 384
ROWS = 192
REACH = 15
HALO = 16
INNER = ROWS - 2 * HALO
STATS = 16
TP = ("xh", "core")
CTX = ("z", "y")
Q_SCALE = math.log2(math.e) / math.sqrt(HEAD)
VMEM_LIMIT = 8 * 2**20
OVERLAPPED = pl.CostEstimate(flops=2 * 10**10, bytes_accessed=2**20, transcendentals=0)


def layer_norm(inputs, gain, eps=1e-05):
    inputs = inputs.astype(jnp.float32)
    average = jnp.mean(inputs, axis=-1, keepdims=True)
    centered = inputs - average
    variance = jnp.mean(centered * centered, axis=-1, keepdims=True)
    return (centered * lax.rsqrt(variance + eps) * gain).astype(jnp.bfloat16)


def split_three(value):
    high = value.astype(jnp.bfloat16).astype(jnp.float32)
    rest = value - high
    mid = rest.astype(jnp.bfloat16).astype(jnp.float32)
    return high, mid, rest - mid


def head_mask(head):
    start = 128 * (head // 2)
    lane = lax.broadcasted_iota(jnp.int32, (1, 256), 1) + start
    return (lane >= head * HEAD) & (lane < (head + 1) * HEAD)


def attend(queries, keys, values, pair):
    start = 128 * pair
    window = queries[:, start : start + 256]
    masks = [head_mask(2 * pair + side) for side in range(2)]
    masked = jnp.concatenate([jnp.where(mask, window, 0) for mask in masks], 0)
    window = jnp.concatenate([block[:, start : start + 256] for block in keys], 0)
    scores = lax.dot_general(
        masked, window, (((1,), (1,)), ((), ())), preferred_element_type=jnp.float32
    )
    top = jnp.max(scores, axis=1, keepdims=True)
    weights = jnp.exp2(scores - top)
    denominator = jnp.sum(weights, axis=1, keepdims=True)
    window = jnp.concatenate([block[:, start : start + 256] for block in values], 0)
    summed = jnp.dot(weights.astype(jnp.bfloat16), window, preferred_element_type=jnp.float32)
    return masks, summed, top, denominator


def widen(part, pair):
    blank = jnp.zeros((part.shape[0], 128), jnp.float32)
    return jnp.concatenate([part, blank] if pair == 0 else [blank, part], 1)


def split_refs(refs, count):
    keys = [ref.at[:, :COLS] for ref in refs[:count]]
    values = [ref.at[:, COLS:] for ref in refs[:count]]
    return keys, values, refs[count:]


def first_attention_kernel(places, blocks, *refs):
    pieces, refs = refs[: len(places)], refs[len(places) :]
    keys, values, rest = split_refs(refs, blocks)
    o_ref, top_ref, sum_ref = rest
    lane = lax.broadcasted_iota(jnp.int32, (1, 128), 1)
    queries = [ref[at * ROWS : (at + 1) * ROWS] for ref, at in zip(pieces, places)]
    queries = jnp.concatenate(queries, 0)
    count = queries.shape[0]
    total = jnp.zeros((count, COLS), jnp.float32)
    tops = jnp.zeros((count, 128), jnp.float32)
    sums = jnp.ones((count, 128), jnp.float32)
    for pair in range(2):
        masks, summed, top, denominator = attend(queries, keys, values, pair)
        both = jnp.where(masks[0], summed[:count], jnp.where(masks[1], summed[count:], 0.0))
        total = total + widen(both, pair)
        for side in range(2):
            rows = slice(side * count, (side + 1) * count)
            tops = jnp.where(lane == 2 * pair + side, top[rows], tops)
            sums = jnp.where(lane == 2 * pair + side, denominator[rows], sums)
    o_ref[...] = total
    top_ref[...] = tops
    sum_ref[...] = sums


def last_attention_kernel(places, blocks, *refs):
    pieces, refs = refs[: len(places)], refs[len(places) :]
    keys, values, rest = split_refs(refs, blocks)
    prior_ref, top_ref, sum_ref, *outs = rest
    lane = lax.broadcasted_iota(jnp.int32, (1, 128), 1)
    queries = [ref[at * ROWS : (at + 1) * ROWS] for ref, at in zip(pieces, places)]
    queries = jnp.concatenate(queries, 0)
    count = queries.shape[0]
    tops = jnp.zeros((count, 128), jnp.float32)
    sums = jnp.zeros((count, 128), jnp.float32)
    products = []
    for pair in range(2):
        masks, summed, top, denominator = attend(queries, keys, values, pair)
        products.append((masks, summed))
        for side in range(2):
            rows = slice(side * count, (side + 1) * count)
            tops = jnp.where(lane == 2 * pair + side, top[rows], tops)
            sums = jnp.where(lane == 2 * pair + side, denominator[rows], sums)
    joint = jnp.maximum(tops, top_ref[...])
    rescale = jnp.exp2(tops - joint)
    prior_rescale = jnp.exp2(top_ref[...] - joint)
    denominator = sums * rescale + sum_ref[...] * prior_rescale
    inverse = 1.0 / denominator
    rescale = rescale * inverse
    prior_rescale = prior_rescale * inverse
    total = jnp.zeros((count, COLS), jnp.float32)
    for pair, (masks, summed) in enumerate(products):
        prior = prior_ref[:, 128 * pair : 128 * pair + 256]
        both = jnp.zeros((count, 256), jnp.float32)
        for side, mask in enumerate(masks):
            head = slice(2 * pair + side, 2 * pair + side + 1)
            part = summed[side * count : (side + 1) * count] * rescale[:, head]
            both = jnp.where(mask, part + prior * prior_rescale[:, head], both)
        total = total + widen(both, pair)
    high, mid, low = split_three(joint + jnp.log2(denominator))
    stats = jnp.where(
        lane < 4, high, jnp.where(lane < 8, pltpu.roll(mid, 4, 1), pltpu.roll(low, 8, 1))
    )
    for place, out in enumerate(outs):
        rows = slice(place * ROWS, (place + 1) * ROWS)
        out[:ROWS] = total[rows].astype(jnp.bfloat16)
        turned = jnp.concatenate([stats[rows], jnp.zeros((256 - ROWS, 128), jnp.float32)], 0)
        turned = jnp.transpose(turned)[:STATS].astype(jnp.bfloat16)
        blank = jnp.zeros((STATS, COLS - 256), jnp.bfloat16)
        out[ROWS:] = jnp.concatenate([turned, blank], 1)


def attention_cost(rows, blocks):
    flops = 2 * 2 * rows * ROWS * blocks * 256 * HEADS_HERE
    return pl.CostEstimate(flops=flops, bytes_accessed=4 * 2**20, transcendentals=0)


def first_attention(queries, blocks):
    places = tuple(at for _, at in queries)
    rows = len(places) * ROWS
    return pl.pallas_call(
        functools.partial(first_attention_kernel, places, len(blocks)),
        out_shape=[
            jax.ShapeDtypeStruct((rows, COLS), jnp.float32),
            jax.ShapeDtypeStruct((rows, 128), jnp.float32),
            jax.ShapeDtypeStruct((rows, 128), jnp.float32),
        ],
        compiler_params=pltpu.CompilerParams(vmem_limit_bytes=VMEM_LIMIT),
        cost_estimate=attention_cost(rows, len(blocks)),
        name="first_attention",
    )(*[query for query, _ in queries], *blocks)


def last_attention(queries, blocks, prior):
    places = tuple(at for _, at in queries)
    rows = len(places) * ROWS
    return pl.pallas_call(
        functools.partial(last_attention_kernel, places, len(blocks)),
        out_shape=[jax.ShapeDtypeStruct((ROWS + STATS, COLS), jnp.bfloat16)] * (rows // ROWS),
        compiler_params=pltpu.CompilerParams(vmem_limit_bytes=VMEM_LIMIT),
        cost_estimate=attention_cost(rows, len(blocks)),
        name="last_attention",
    )(*[query for query, _ in queries], *blocks, *prior)


def combine_kernel(*refs):
    parts, o_ref = refs[:4], refs[-1]
    lane = lax.broadcasted_iota(jnp.int32, (1, COLS), 1)
    logs = []
    for part in parts:
        stats = part[ROWS:, :256].astype(jnp.float32)
        logs.append(stats[0:4] + stats[4:8] + stats[8:12])
    top = functools.reduce(jnp.maximum, logs)
    shares = [jnp.exp2(log - top) for log in logs]
    inverse = 1.0 / functools.reduce(jnp.add, shares)
    shares = jnp.concatenate([share * inverse for share in shares], 0)
    blank = jnp.zeros((128 - shares.shape[0], 256), jnp.float32)
    shares = jnp.transpose(jnp.concatenate([shares, blank], 0))[:ROWS]
    total = jnp.zeros((ROWS, COLS), jnp.float32)
    for place, part in enumerate(parts):
        spread = jnp.zeros((ROWS, COLS), jnp.float32)
        for head in range(HEADS_HERE):
            inside = (lane >= head * HEAD) & (lane < (head + 1) * HEAD)
            column = place * HEADS_HERE + head
            spread = jnp.where(inside, shares[:, column : column + 1], spread)
        total = total + spread * part[:ROWS].astype(jnp.float32)
    o_ref[...] = total.astype(jnp.bfloat16)


def combine(parts, others):
    vmem = pl.BlockSpec(memory_space=pltpu.VMEM)
    anywhere = pl.BlockSpec(memory_space=pl.ANY)
    return pl.pallas_call(
        combine_kernel,
        in_specs=[vmem] * len(parts) + [anywhere] * len(others),
        out_specs=vmem,
        out_shape=jax.ShapeDtypeStruct((ROWS, COLS), jnp.bfloat16),
        compiler_params=pltpu.CompilerParams(vmem_limit_bytes=VMEM_LIMIT),
        cost_estimate=OVERLAPPED,
        name="combine",
    )(*parts, *others)


def middle_kernel(
    rows_ref, context_ref, w0, w1, w2, w3, gain_ref, glu_ref, other_ref, m_ref, g_ref, top_ref, end_ref
):
    place = lax.axis_index(TP)
    total = rows_ref[...].astype(jnp.float32)
    for offset, weight in enumerate((w0, w1, w2, w3)):
        total = total + jnp.dot(
            context_ref[place ^ offset], weight[...], preferred_element_type=jnp.float32
        )
    middle = total.astype(jnp.bfloat16)
    for position in range(4):

        @pl.when(place == position)
        def _():
            m_ref[...] = middle[:, position * COLS : (position + 1) * COLS]

    normed = layer_norm(middle, gain_ref[...].reshape(1, D))
    for half, weight in enumerate((glu_ref, other_ref)):
        value = jnp.dot(normed, weight[0], preferred_element_type=jnp.float32)
        gate = jnp.dot(normed, weight[1], preferred_element_type=jnp.float32)
        glu = (value * (1.0 / (1.0 + jnp.exp(-gate)))).astype(jnp.bfloat16)
        here = slice(half * COLS, (half + 1) * COLS)
        g_ref[:, here] = glu
        top_ref[:, here] = glu[:HALO]
        end_ref[:, here] = glu[ROWS - HALO :]


def middle_and_glu(rows, context, weights, gain, glu_weight, glu_other):
    vmem = pl.BlockSpec(memory_space=pltpu.VMEM)
    return pl.pallas_call(
        middle_kernel,
        in_specs=[vmem] * 9,
        out_specs=[vmem] * 4,
        out_shape=[
            jax.ShapeDtypeStruct((ROWS, COLS), jnp.bfloat16),
            jax.ShapeDtypeStruct((ROWS, 2 * COLS), jnp.bfloat16),
            jax.ShapeDtypeStruct((HALO, 2 * COLS), jnp.bfloat16),
            jax.ShapeDtypeStruct((HALO, 2 * COLS), jnp.bfloat16),
        ],
        compiler_params=pltpu.CompilerParams(vmem_limit_bytes=VMEM_LIMIT),
        cost_estimate=OVERLAPPED,
        name="middle",
    )(rows, context, *weights, gain, glu_weight, glu_other)


def convolve(held, filters, count, store):
    for half, (taps_ref, bias_ref) in enumerate(filters):
        taps = taps_ref[...].astype(jnp.float32)
        for column in range(COLS // 128):
            local = slice(column * 128, (column + 1) * 128)
            here = slice(half * COLS + column * 128, half * COLS + (column + 1) * 128)
            total = jnp.zeros((count, 128), jnp.float32) + bias_ref[local].reshape(1, 128)
            for offset in range(8):
                group = jnp.zeros((count + 8, 128), jnp.float32)
                for begin in range(offset, 2 * HALO, 8):
                    tap = begin - (HALO - REACH)
                    if tap >= 0:
                        aligned = held[begin - offset : begin - offset + count + 8, here]
                        group = group + aligned * taps[tap : tap + 1, local]
                total = total + group[offset : offset + count]
            store(here, (total / (1.0 + jnp.exp(-total))).astype(jnp.bfloat16))


def inner_kernel(glu_ref, taps0, bias0, taps1, bias1, o_ref, held):
    held[...] = glu_ref[...].astype(jnp.float32)

    def store(here, value):
        o_ref[:, here] = value

    convolve(held, ((taps0, bias0), (taps1, bias1)), INNER, store)


def edges_kernel(before_ref, glu_ref, after_ref, taps0, bias0, taps1, bias1, o_ref, held):
    for side in range(2):
        if side == 0:
            held[:HALO] = before_ref[...].astype(jnp.float32)
            held[HALO:] = glu_ref[: 2 * HALO].astype(jnp.float32)
        else:
            held[: 2 * HALO] = glu_ref[ROWS - 2 * HALO :].astype(jnp.float32)
            held[2 * HALO :] = after_ref[...].astype(jnp.float32)

        def store(here, value):
            o_ref[side * HALO : (side + 1) * HALO, here] = value

        convolve(held, ((taps0, bias0), (taps1, bias1)), HALO, store)


def conv_inner(glu, filters):
    return pl.pallas_call(
        inner_kernel,
        out_shape=jax.ShapeDtypeStruct((INNER, 2 * COLS), jnp.bfloat16),
        scratch_shapes=[pltpu.VMEM((ROWS, 2 * COLS), jnp.float32)],
        compiler_params=pltpu.CompilerParams(vmem_limit_bytes=VMEM_LIMIT),
        name="inner",
    )(glu, *filters)


def conv_edges(before, glu, after, filters):
    return pl.pallas_call(
        edges_kernel,
        out_shape=jax.ShapeDtypeStruct((2 * HALO, 2 * COLS), jnp.bfloat16),
        scratch_shapes=[pltpu.VMEM((3 * HALO, 2 * COLS), jnp.float32)],
        compiler_params=pltpu.CompilerParams(vmem_limit_bytes=VMEM_LIMIT),
        cost_estimate=OVERLAPPED,
        name="edges",
    )(before, glu, after, *filters)


def project_kernel(eps_ref, rows_ref, gain_ref, w_ref, kv_ref, q_ref):
    normed = layer_norm(rows_ref[...], gain_ref[...].reshape(1, D), eps_ref[0:1, 0:1])
    for half in range(2):
        kv_ref[:, half * COLS : (half + 1) * COLS] = jnp.dot(
            normed, w_ref[1 + half], preferred_element_type=jnp.float32
        ).astype(jnp.bfloat16)
    query = jnp.dot(normed, w_ref[0], preferred_element_type=jnp.float32)
    q_ref[...] = (query * Q_SCALE).astype(jnp.bfloat16)


def project(eps, rows, gain, weights):
    return pl.pallas_call(
        project_kernel,
        out_shape=[
            jax.ShapeDtypeStruct((ROWS, 2 * COLS), jnp.bfloat16),
            jax.ShapeDtypeStruct((ROWS, COLS), jnp.bfloat16),
        ],
        compiler_params=pltpu.CompilerParams(vmem_limit_bytes=VMEM_LIMIT),
        name="project",
    )(eps, rows, gain, weights)


def epsilon_kernel(o_ref):
    o_ref[...] = jnp.full((8, 128), 1e-05, jnp.float32)


def epsilon():
    return pl.pallas_call(
        epsilon_kernel,
        out_shape=jax.ShapeDtypeStruct((8, 128), jnp.float32),
        compiler_params=pltpu.CompilerParams(vmem_limit_bytes=VMEM_LIMIT),
        cost_estimate=OVERLAPPED,
        name="epsilon",
    )()


def join_kernel(a_ref, b_ref, _, o_ref):
    o_ref[:ROWS] = a_ref[...]
    o_ref[ROWS:] = b_ref[...]


def join(a, b, other):
    vmem = pl.BlockSpec(memory_space=pltpu.VMEM)
    return pl.pallas_call(
        join_kernel,
        in_specs=[vmem, vmem, pl.BlockSpec(memory_space=pl.ANY)],
        out_shape=jax.ShapeDtypeStruct((2 * ROWS, COLS), jnp.bfloat16),
        compiler_params=pltpu.CompilerParams(vmem_limit_bytes=VMEM_LIMIT),
        name="join",
    )(a, b, other)


def halves_kernel(a_ref, b_ref, _, a_out, b_out):
    a_out[...] = a_ref[: ROWS // 2]
    b_out[...] = b_ref[ROWS // 2 :]


def halves(a, b, other):
    vmem = pl.BlockSpec(memory_space=pltpu.VMEM)
    return pl.pallas_call(
        halves_kernel,
        in_specs=[vmem, vmem, pl.BlockSpec(memory_space=pl.ANY)],
        out_shape=[jax.ShapeDtypeStruct((ROWS // 2, 2 * COLS), jnp.bfloat16)] * 2,
        compiler_params=pltpu.CompilerParams(vmem_limit_bytes=VMEM_LIMIT),
        name="halves",
    )(a, b, other)


def product(flip, act_ref, w_own, w_other):
    columns = pl.ds(pl.multiple_of((lax.axis_index(TP) ^ flip) * COLS, 128), COLS)
    total = jnp.dot(act_ref[:, :COLS], w_own[:, columns], preferred_element_type=jnp.float32)
    return total + jnp.dot(
        act_ref[:, COLS:], w_other[:, columns], preferred_element_type=jnp.float32
    )


def part_kernel(flip, act_ref, w_own, w_other, o_ref):
    o_ref[...] = product(flip, act_ref, w_own, w_other).astype(o_ref.dtype)


def part_sum(flip, act, weights, kind):
    return pl.pallas_call(
        functools.partial(part_kernel, flip),
        out_shape=jax.ShapeDtypeStruct((act.shape[0], COLS), kind),
        compiler_params=pltpu.CompilerParams(vmem_limit_bytes=VMEM_LIMIT),
        name="part_sum",
    )(act, *weights)


def final_kernel(act_ref, w_own, w_other, middle_ref, ours_ref, inner_ref, edges_ref, o_ref):
    here = slice(HALO, HALO + INNER)
    total = ours_ref[...] + inner_ref[...].astype(jnp.float32)
    o_ref[here] = (middle_ref[here].astype(jnp.float32) + total).astype(jnp.bfloat16)
    total = product(0, act_ref, w_own, w_other) + edges_ref[...].astype(jnp.float32)
    for side in range(2):
        here = slice(side * (ROWS - HALO), side * (ROWS - HALO) + HALO)
        part = total[side * HALO : (side + 1) * HALO]
        o_ref[here] = (middle_ref[here].astype(jnp.float32) + part).astype(jnp.bfloat16)


def final(act, weights, middle, ours, inner, edges):
    return pl.pallas_call(
        final_kernel,
        out_shape=jax.ShapeDtypeStruct((ROWS, COLS), jnp.bfloat16),
        compiler_params=pltpu.CompilerParams(vmem_limit_bytes=VMEM_LIMIT),
        name="final",
    )(act, *weights, middle, ours, inner, edges)


def swap(value, axis, count, flip):
    return lax.ppermute(value, axis, [(i, i ^ flip) for i in range(count)])


def shift(value, axis, count, offset):
    return lax.ppermute(value, axis, [(i, (i + offset) % count) for i in range(count)])


def per_device(
    frames,
    attn_gain,
    query_key_value,
    out_weight,
    conv_gain,
    glu_weight,
    depth_kernel,
    depth_bias,
    proj_weight,
):
    out_core = swap(out_weight, "core", 2, 1)
    glu_core = swap(glu_weight, "core", 2, 1)
    out_far = swap(out_weight, "xh", 2, 1)
    whole_rows = lax.all_gather(frames, TP, axis=1, tiled=True)
    mine, query = project(epsilon(), whole_rows, attn_gain, query_key_value)
    lower1, upper1 = shift(mine, "z", 8, 1), shift(mine, "z", 8, -1)
    query1 = swap(query, "y", 4, 1)
    lower2, upper2 = shift(lower1, "z", 8, 1), shift(upper1, "z", 8, -1)
    pair2 = swap(join(query, query1, out_core), "y", 4, 2)
    low_half, high_half = halves(lower2, upper2, glu_core)
    second = [
        shift(lower2, "z", 8, 1),
        shift(upper2, "z", 8, -1),
        shift(low_half, "z", 8, 2),
        shift(high_half, "z", 8, -2),
    ]
    blocks = [mine, lower1, upper1, lower2, upper2]
    groups = ([(pair2, 0)], [(query1, 0), (pair2, 1)], [(query, 0)])
    priors = [first_attention(group, blocks) for group in groups]
    (partial2,) = last_attention(groups[0], second, priors[0])
    part2 = swap(partial2, "y", 4, 2)
    partial1, partial3 = last_attention(groups[1], second, priors[1])
    part1, part3 = swap(partial1, "y", 4, 1), swap(partial3, "y", 4, 3)
    (partial0,) = last_attention(groups[2], second, priors[2])
    out_far_core = swap(out_far, "core", 2, 1)
    out_pieces = (out_weight, out_core, out_far, out_far_core)
    taps_core = swap(depth_kernel, "core", 2, 1)
    bias_core = swap(depth_bias, "core", 2, 1)
    context = combine([partial0, part1, part2, part3], [taps_core, bias_core])
    proj_core = swap(proj_weight, "core", 2, 1)
    context = lax.all_gather(context, TP, axis=0, tiled=False)
    middle, glu, top, end = middle_and_glu(
        whole_rows, context, out_pieces, conv_gain, glu_weight, glu_core
    )
    before = lax.ppermute(end, CTX, [(i, i + 1) for i in range(31)])
    after = lax.ppermute(top, CTX, [(i + 1, i) for i in range(31)])
    weights = (proj_weight, proj_core)
    filters = (depth_kernel, depth_bias, taps_core, bias_core)
    inner = conv_inner(glu, filters)
    inner_far = swap(part_sum(2, inner, weights, jnp.bfloat16), "xh", 2, 1)
    ours = part_sum(0, inner, weights, jnp.float32)
    edges = conv_edges(before, glu, after, filters)
    edges_far = swap(part_sum(2, edges, weights, jnp.bfloat16), "xh", 2, 1)
    return final(edges, weights, middle, ours, inner_far, edges_far)


def solution(mesh):
    parted = Mesh(mesh.devices.reshape(2, 8, 4, 2, 2), ("batch", "z", "y", "xh", "core"))
    in_specs = (
        P(("batch",) + CTX, TP),
        P(),
        P(None, None, TP),
        P(TP, None),
        P(),
        P(None, None, TP),
        P(None, TP),
        P(TP),
        P(TP, None),
    )
    out_specs = P(("batch",) + CTX, TP)
    return jax.shard_map(
        per_device, mesh=parted, in_specs=in_specs, out_specs=out_specs, check_vma=False
    )
```

```python
import functools
import math

import jax
import jax.numpy as jnp
from jax import lax
from jax.experimental import pallas as pl
from jax.experimental.pallas import tpu as pltpu
from jax.sharding import Mesh
from jax.sharding import PartitionSpec as P

D = 1536
HEAD = 96
HEADS_HERE = 4
COLS = 384
ROWS = 192
REACH = 15
HALO = 16
INNER = ROWS - 2 * HALO
STATS = 16
TP = ("xh", "core")
CTX = ("z", "y")
Q_SCALE = math.log2(math.e) / math.sqrt(HEAD)
VMEM_LIMIT = 8 * 2**20
OVERLAPPED = pl.CostEstimate(flops=2 * 10**10, bytes_accessed=2**20, transcendentals=0)


def layer_norm(inputs, gain, eps=1e-05):
    inputs = inputs.astype(jnp.float32)
    average = jnp.mean(inputs, axis=-1, keepdims=True)
    centered = inputs - average
    variance = jnp.mean(centered * centered, axis=-1, keepdims=True)
    return (centered * lax.rsqrt(variance + eps) * gain).astype(jnp.bfloat16)


def split_three(value):
    high = value.astype(jnp.bfloat16).astype(jnp.float32)
    rest = value - high
    mid = rest.astype(jnp.bfloat16).astype(jnp.float32)
    return high, mid, rest - mid


def head_mask(head):
    start = 128 * (head // 2)
    lane = lax.broadcasted_iota(jnp.int32, (1, 256), 1) + start
    return (lane >= head * HEAD) & (lane < (head + 1) * HEAD)


def attend(queries, keys, values, pair):
    start = 128 * pair
    window = queries[:, start : start + 256]
    masks = [head_mask(2 * pair + side) for side in range(2)]
    masked = jnp.concatenate([jnp.where(mask, window, 0) for mask in masks], 0)
    window = jnp.concatenate([block[:, start : start + 256] for block in keys], 0)
    scores = lax.dot_general(
        masked, window, (((1,), (1,)), ((), ())), preferred_element_type=jnp.float32
    )
    top = jnp.max(scores, axis=1, keepdims=True)
    weights = jnp.exp2(scores - top)
    denominator = jnp.sum(weights, axis=1, keepdims=True)
    window = jnp.concatenate([block[:, start : start + 256] for block in values], 0)
    summed = jnp.dot(weights.astype(jnp.bfloat16), window, preferred_element_type=jnp.float32)
    return masks, summed, top, denominator


def widen(part, pair):
    blank = jnp.zeros((part.shape[0], 128), jnp.float32)
    return jnp.concatenate([part, blank] if pair == 0 else [blank, part], 1)


def split_refs(refs, count):
    keys = [ref.at[:, :COLS] for ref in refs[:count]]
    values = [ref.at[:, COLS:] for ref in refs[:count]]
    return keys, values, refs[count:]


def first_attention_kernel(places, blocks, *refs):
    pieces, refs = refs[: len(places)], refs[len(places) :]
    keys, values, rest = split_refs(refs, blocks)
    o_ref, top_ref, sum_ref = rest
    lane = lax.broadcasted_iota(jnp.int32, (1, 128), 1)
    queries = [ref[at * ROWS : (at + 1) * ROWS] for ref, at in zip(pieces, places)]
    queries = jnp.concatenate(queries, 0)
    count = queries.shape[0]
    total = jnp.zeros((count, COLS), jnp.float32)
    tops = jnp.zeros((count, 128), jnp.float32)
    sums = jnp.ones((count, 128), jnp.float32)
    for pair in range(2):
        masks, summed, top, denominator = attend(queries, keys, values, pair)
        both = jnp.where(masks[0], summed[:count], jnp.where(masks[1], summed[count:], 0.0))
        total = total + widen(both, pair)
        for side in range(2):
            rows = slice(side * count, (side + 1) * count)
            tops = jnp.where(lane == 2 * pair + side, top[rows], tops)
            sums = jnp.where(lane == 2 * pair + side, denominator[rows], sums)
    o_ref[...] = total
    top_ref[...] = tops
    sum_ref[...] = sums


def last_attention_kernel(places, blocks, *refs):
    pieces, refs = refs[: len(places)], refs[len(places) :]
    keys, values, rest = split_refs(refs, blocks)
    prior_ref, top_ref, sum_ref, *outs = rest
    lane = lax.broadcasted_iota(jnp.int32, (1, 128), 1)
    queries = [ref[at * ROWS : (at + 1) * ROWS] for ref, at in zip(pieces, places)]
    queries = jnp.concatenate(queries, 0)
    count = queries.shape[0]
    tops = jnp.zeros((count, 128), jnp.float32)
    sums = jnp.zeros((count, 128), jnp.float32)
    products = []
    for pair in range(2):
        masks, summed, top, denominator = attend(queries, keys, values, pair)
        products.append((masks, summed))
        for side in range(2):
            rows = slice(side * count, (side + 1) * count)
            tops = jnp.where(lane == 2 * pair + side, top[rows], tops)
            sums = jnp.where(lane == 2 * pair + side, denominator[rows], sums)
    joint = jnp.maximum(tops, top_ref[...])
    rescale = jnp.exp2(tops - joint)
    prior_rescale = jnp.exp2(top_ref[...] - joint)
    denominator = sums * rescale + sum_ref[...] * prior_rescale
    inverse = 1.0 / denominator
    rescale = rescale * inverse
    prior_rescale = prior_rescale * inverse
    total = jnp.zeros((count, COLS), jnp.float32)
    for pair, (masks, summed) in enumerate(products):
        prior = prior_ref[:, 128 * pair : 128 * pair + 256]
        both = jnp.zeros((count, 256), jnp.float32)
        for side, mask in enumerate(masks):
            head = slice(2 * pair + side, 2 * pair + side + 1)
            part = summed[side * count : (side + 1) * count] * rescale[:, head]
            both = jnp.where(mask, part + prior * prior_rescale[:, head], both)
        total = total + widen(both, pair)
    high, mid, low = split_three(joint + jnp.log2(denominator))
    stats = jnp.where(
        lane < 4, high, jnp.where(lane < 8, pltpu.roll(mid, 4, 1), pltpu.roll(low, 8, 1))
    )
    for place, out in enumerate(outs):
        rows = slice(place * ROWS, (place + 1) * ROWS)
        out[:ROWS] = total[rows].astype(jnp.bfloat16)
        turned = jnp.concatenate([stats[rows], jnp.zeros((256 - ROWS, 128), jnp.float32)], 0)
        turned = jnp.transpose(turned)[:STATS].astype(jnp.bfloat16)
        blank = jnp.zeros((STATS, COLS - 256), jnp.bfloat16)
        out[ROWS:] = jnp.concatenate([turned, blank], 1)


def attention_cost(rows, blocks):
    flops = 2 * 2 * rows * ROWS * blocks * 256 * HEADS_HERE
    return pl.CostEstimate(flops=flops, bytes_accessed=4 * 2**20, transcendentals=0)


def first_attention(queries, blocks):
    places = tuple(at for _, at in queries)
    rows = len(places) * ROWS
    return pl.pallas_call(
        functools.partial(first_attention_kernel, places, len(blocks)),
        out_shape=[
            jax.ShapeDtypeStruct((rows, COLS), jnp.float32),
            jax.ShapeDtypeStruct((rows, 128), jnp.float32),
            jax.ShapeDtypeStruct((rows, 128), jnp.float32),
        ],
        compiler_params=pltpu.CompilerParams(vmem_limit_bytes=VMEM_LIMIT),
        cost_estimate=attention_cost(rows, len(blocks)),
        name="first_attention",
    )(*[query for query, _ in queries], *blocks)


def last_attention(queries, blocks, prior):
    places = tuple(at for _, at in queries)
    rows = len(places) * ROWS
    return pl.pallas_call(
        functools.partial(last_attention_kernel, places, len(blocks)),
        out_shape=[jax.ShapeDtypeStruct((ROWS + STATS, COLS), jnp.bfloat16)] * (rows // ROWS),
        compiler_params=pltpu.CompilerParams(vmem_limit_bytes=VMEM_LIMIT),
        cost_estimate=attention_cost(rows, len(blocks)),
        name="last_attention",
    )(*[query for query, _ in queries], *blocks, *prior)


def combine_kernel(*refs):
    parts, o_ref = refs[:4], refs[-1]
    lane = lax.broadcasted_iota(jnp.int32, (1, COLS), 1)
    logs = []
    for part in parts:
        stats = part[ROWS:, :256].astype(jnp.float32)
        logs.append(stats[0:4] + stats[4:8] + stats[8:12])
    top = functools.reduce(jnp.maximum, logs)
    shares = [jnp.exp2(log - top) for log in logs]
    inverse = 1.0 / functools.reduce(jnp.add, shares)
    shares = jnp.concatenate([share * inverse for share in shares], 0)
    blank = jnp.zeros((128 - shares.shape[0], 256), jnp.float32)
    shares = jnp.transpose(jnp.concatenate([shares, blank], 0))[:ROWS]
    total = jnp.zeros((ROWS, COLS), jnp.float32)
    for place, part in enumerate(parts):
        spread = jnp.zeros((ROWS, COLS), jnp.float32)
        for head in range(HEADS_HERE):
            inside = (lane >= head * HEAD) & (lane < (head + 1) * HEAD)
            column = place * HEADS_HERE + head
            spread = jnp.where(inside, shares[:, column : column + 1], spread)
        total = total + spread * part[:ROWS].astype(jnp.float32)
    o_ref[...] = total.astype(jnp.bfloat16)


def combine(parts, others):
    vmem = pl.BlockSpec(memory_space=pltpu.VMEM)
    anywhere = pl.BlockSpec(memory_space=pl.ANY)
    return pl.pallas_call(
        combine_kernel,
        in_specs=[vmem] * len(parts) + [anywhere] * len(others),
        out_specs=vmem,
        out_shape=jax.ShapeDtypeStruct((ROWS, COLS), jnp.bfloat16),
        compiler_params=pltpu.CompilerParams(vmem_limit_bytes=VMEM_LIMIT),
        cost_estimate=OVERLAPPED,
        name="combine",
    )(*parts, *others)


def middle_kernel(
    rows_ref, context_ref, w0, w1, w2, w3, gain_ref, glu_ref, other_ref, m_ref, g_ref, top_ref, end_ref
):
    place = lax.axis_index(TP)
    total = rows_ref[...].astype(jnp.float32)
    for offset, weight in enumerate((w0, w1, w2, w3)):
        total = total + jnp.dot(
            context_ref[place ^ offset], weight[...], preferred_element_type=jnp.float32
        )
    middle = total.astype(jnp.bfloat16)
    for position in range(4):

        @pl.when(place == position)
        def _():
            m_ref[...] = middle[:, position * COLS : (position + 1) * COLS]

    normed = layer_norm(middle, gain_ref[...].reshape(1, D))
    for half, weight in enumerate((glu_ref, other_ref)):
        value = jnp.dot(normed, weight[0], preferred_element_type=jnp.float32)
        gate = jnp.dot(normed, weight[1], preferred_element_type=jnp.float32)
        glu = (value * (1.0 / (1.0 + jnp.exp(-gate)))).astype(jnp.bfloat16)
        here = slice(half * COLS, (half + 1) * COLS)
        g_ref[:, here] = glu
        top_ref[:, here] = glu[:HALO]
        end_ref[:, here] = glu[ROWS - HALO :]


def middle_and_glu(rows, context, weights, gain, glu_weight, glu_other):
    vmem = pl.BlockSpec(memory_space=pltpu.VMEM)
    return pl.pallas_call(
        middle_kernel,
        in_specs=[vmem] * 9,
        out_specs=[vmem] * 4,
        out_shape=[
            jax.ShapeDtypeStruct((ROWS, COLS), jnp.bfloat16),
            jax.ShapeDtypeStruct((ROWS, 2 * COLS), jnp.bfloat16),
            jax.ShapeDtypeStruct((HALO, 2 * COLS), jnp.bfloat16),
            jax.ShapeDtypeStruct((HALO, 2 * COLS), jnp.bfloat16),
        ],
        compiler_params=pltpu.CompilerParams(vmem_limit_bytes=VMEM_LIMIT),
        cost_estimate=OVERLAPPED,
        name="middle",
    )(rows, context, *weights, gain, glu_weight, glu_other)


def convolve(held, filters, count, store):
    for half, (taps_ref, bias_ref) in enumerate(filters):
        taps = taps_ref[...].astype(jnp.float32)
        for column in range(COLS // 128):
            local = slice(column * 128, (column + 1) * 128)
            here = slice(half * COLS + column * 128, half * COLS + (column + 1) * 128)
            total = jnp.zeros((count, 128), jnp.float32) + bias_ref[local].reshape(1, 128)
            for offset in range(8):
                group = jnp.zeros((count + 8, 128), jnp.float32)
                for begin in range(offset, 2 * HALO, 8):
                    tap = begin - (HALO - REACH)
                    if tap >= 0:
                        aligned = held[begin - offset : begin - offset + count + 8, here]
                        group = group + aligned * taps[tap : tap + 1, local]
                total = total + group[offset : offset + count]
            store(here, (total / (1.0 + jnp.exp(-total))).astype(jnp.bfloat16))


def inner_kernel(glu_ref, taps0, bias0, taps1, bias1, o_ref, held):
    held[...] = glu_ref[...].astype(jnp.float32)

    def store(here, value):
        o_ref[:, here] = value

    convolve(held, ((taps0, bias0), (taps1, bias1)), INNER, store)


def edges_kernel(before_ref, glu_ref, after_ref, taps0, bias0, taps1, bias1, o_ref, held):
    for side in range(2):
        if side == 0:
            held[:HALO] = before_ref[...].astype(jnp.float32)
            held[HALO:] = glu_ref[: 2 * HALO].astype(jnp.float32)
        else:
            held[: 2 * HALO] = glu_ref[ROWS - 2 * HALO :].astype(jnp.float32)
            held[2 * HALO :] = after_ref[...].astype(jnp.float32)

        def store(here, value):
            o_ref[side * HALO : (side + 1) * HALO, here] = value

        convolve(held, ((taps0, bias0), (taps1, bias1)), HALO, store)


def conv_inner(glu, filters):
    return pl.pallas_call(
        inner_kernel,
        out_shape=jax.ShapeDtypeStruct((INNER, 2 * COLS), jnp.bfloat16),
        scratch_shapes=[pltpu.VMEM((ROWS, 2 * COLS), jnp.float32)],
        compiler_params=pltpu.CompilerParams(vmem_limit_bytes=VMEM_LIMIT),
        name="inner",
    )(glu, *filters)


def conv_edges(before, glu, after, filters):
    return pl.pallas_call(
        edges_kernel,
        out_shape=jax.ShapeDtypeStruct((2 * HALO, 2 * COLS), jnp.bfloat16),
        scratch_shapes=[pltpu.VMEM((3 * HALO, 2 * COLS), jnp.float32)],
        compiler_params=pltpu.CompilerParams(vmem_limit_bytes=VMEM_LIMIT),
        cost_estimate=OVERLAPPED,
        name="edges",
    )(before, glu, after, *filters)


def project_kernel(eps_ref, rows_ref, gain_ref, w_ref, kv_ref, q_ref):
    normed = layer_norm(rows_ref[...], gain_ref[...].reshape(1, D), eps_ref[0:1, 0:1])
    for half in range(2):
        kv_ref[:, half * COLS : (half + 1) * COLS] = jnp.dot(
            normed, w_ref[1 + half], preferred_element_type=jnp.float32
        ).astype(jnp.bfloat16)
    query = jnp.dot(normed, w_ref[0], preferred_element_type=jnp.float32)
    q_ref[...] = (query * Q_SCALE).astype(jnp.bfloat16)


def project(eps, rows, gain, weights):
    return pl.pallas_call(
        project_kernel,
        out_shape=[
            jax.ShapeDtypeStruct((ROWS, 2 * COLS), jnp.bfloat16),
            jax.ShapeDtypeStruct((ROWS, COLS), jnp.bfloat16),
        ],
        compiler_params=pltpu.CompilerParams(vmem_limit_bytes=VMEM_LIMIT),
        name="project",
    )(eps, rows, gain, weights)


def epsilon_kernel(o_ref):
    o_ref[...] = jnp.full((8, 128), 1e-05, jnp.float32)


def epsilon():
    return pl.pallas_call(
        epsilon_kernel,
        out_shape=jax.ShapeDtypeStruct((8, 128), jnp.float32),
        compiler_params=pltpu.CompilerParams(vmem_limit_bytes=VMEM_LIMIT),
        cost_estimate=OVERLAPPED,
        name="epsilon",
    )()


def join_kernel(a_ref, b_ref, _, o_ref):
    o_ref[:ROWS] = a_ref[...]
    o_ref[ROWS:] = b_ref[...]


def join(a, b, other):
    vmem = pl.BlockSpec(memory_space=pltpu.VMEM)
    return pl.pallas_call(
        join_kernel,
        in_specs=[vmem, vmem, pl.BlockSpec(memory_space=pl.ANY)],
        out_shape=jax.ShapeDtypeStruct((2 * ROWS, COLS), jnp.bfloat16),
        compiler_params=pltpu.CompilerParams(vmem_limit_bytes=VMEM_LIMIT),
        name="join",
    )(a, b, other)


def halves_kernel(a_ref, b_ref, _, a_out, b_out):
    a_out[...] = a_ref[: ROWS // 2]
    b_out[...] = b_ref[ROWS // 2 :]


def halves(a, b, other):
    vmem = pl.BlockSpec(memory_space=pltpu.VMEM)
    return pl.pallas_call(
        halves_kernel,
        in_specs=[vmem, vmem, pl.BlockSpec(memory_space=pl.ANY)],
        out_shape=[jax.ShapeDtypeStruct((ROWS // 2, 2 * COLS), jnp.bfloat16)] * 2,
        compiler_params=pltpu.CompilerParams(vmem_limit_bytes=VMEM_LIMIT),
        name="halves",
    )(a, b, other)


def product(flip, act_ref, w_own, w_other):
    columns = pl.ds(pl.multiple_of((lax.axis_index(TP) ^ flip) * COLS, 128), COLS)
    total = jnp.dot(act_ref[:, :COLS], w_own[:, columns], preferred_element_type=jnp.float32)
    return total + jnp.dot(
        act_ref[:, COLS:], w_other[:, columns], preferred_element_type=jnp.float32
    )


def part_kernel(flip, act_ref, w_own, w_other, o_ref):
    o_ref[...] = product(flip, act_ref, w_own, w_other).astype(o_ref.dtype)


def part_sum(flip, act, weights, kind):
    return pl.pallas_call(
        functools.partial(part_kernel, flip),
        out_shape=jax.ShapeDtypeStruct((act.shape[0], COLS), kind),
        compiler_params=pltpu.CompilerParams(vmem_limit_bytes=VMEM_LIMIT),
        name="part_sum",
    )(act, *weights)


def final_kernel(middle_ref, ours_ref, ours_edges_ref, inner_ref, edges_ref, o_ref):
    here = slice(HALO, HALO + INNER)
    total = ours_ref[...] + inner_ref[...].astype(jnp.float32)
    o_ref[here] = (middle_ref[here].astype(jnp.float32) + total).astype(jnp.bfloat16)
    total = ours_edges_ref[...] + edges_ref[...].astype(jnp.float32)
    for side in range(2):
        here = slice(side * (ROWS - HALO), side * (ROWS - HALO) + HALO)
        part = total[side * HALO : (side + 1) * HALO]
        o_ref[here] = (middle_ref[here].astype(jnp.float32) + part).astype(jnp.bfloat16)


def final(middle, ours, ours_edges, inner, edges):
    return pl.pallas_call(
        final_kernel,
        out_shape=jax.ShapeDtypeStruct((ROWS, COLS), jnp.bfloat16),
        compiler_params=pltpu.CompilerParams(vmem_limit_bytes=VMEM_LIMIT),
        name="final",
    )(middle, ours, ours_edges, inner, edges)


def swap(value, axis, count, flip):
    return lax.ppermute(value, axis, [(i, i ^ flip) for i in range(count)])


def shift(value, axis, count, offset):
    return lax.ppermute(value, axis, [(i, (i + offset) % count) for i in range(count)])


def per_device(
    frames,
    attn_gain,
    query_key_value,
    out_weight,
    conv_gain,
    glu_weight,
    depth_kernel,
    depth_bias,
    proj_weight,
):
    out_core = swap(out_weight, "core", 2, 1)
    glu_core = swap(glu_weight, "core", 2, 1)
    out_far = swap(out_weight, "xh", 2, 1)
    whole_rows = lax.all_gather(frames, TP, axis=1, tiled=True)
    mine, query = project(epsilon(), whole_rows, attn_gain, query_key_value)
    lower1, upper1 = shift(mine, "z", 8, 1), shift(mine, "z", 8, -1)
    query1 = swap(query, "y", 4, 1)
    lower2, upper2 = shift(lower1, "z", 8, 1), shift(upper1, "z", 8, -1)
    pair2 = swap(join(query, query1, out_core), "y", 4, 2)
    low_half, high_half = halves(lower2, upper2, glu_core)
    second = [
        shift(lower2, "z", 8, 1),
        shift(upper2, "z", 8, -1),
        shift(low_half, "z", 8, 2),
        shift(high_half, "z", 8, -2),
    ]
    blocks = [mine, lower1, upper1, lower2, upper2]
    groups = ([(pair2, 0)], [(query1, 0), (pair2, 1)], [(query, 0)])
    priors = [first_attention(group, blocks) for group in groups]
    (partial2,) = last_attention(groups[0], second, priors[0])
    part2 = swap(partial2, "y", 4, 2)
    partial1, partial3 = last_attention(groups[1], second, priors[1])
    part1, part3 = swap(partial1, "y", 4, 1), swap(partial3, "y", 4, 3)
    (partial0,) = last_attention(groups[2], second, priors[2])
    out_far_core = swap(out_far, "core", 2, 1)
    out_pieces = (out_weight, out_core, out_far, out_far_core)
    taps_core = swap(depth_kernel, "core", 2, 1)
    bias_core = swap(depth_bias, "core", 2, 1)
    context = combine([partial0, part1, part2, part3], [taps_core, bias_core])
    proj_core = swap(proj_weight, "core", 2, 1)
    context = lax.all_gather(context, TP, axis=0, tiled=False)
    middle, glu, top, end = middle_and_glu(
        whole_rows, context, out_pieces, conv_gain, glu_weight, glu_core
    )
    before = lax.ppermute(end, CTX, [(i, i + 1) for i in range(31)])
    after = lax.ppermute(top, CTX, [(i + 1, i) for i in range(31)])
    weights = (proj_weight, proj_core)
    filters = (depth_kernel, depth_bias, taps_core, bias_core)
    inner = conv_inner(glu, filters)
    inner_far = swap(part_sum(2, inner, weights, jnp.bfloat16), "xh", 2, 1)
    ours = part_sum(0, inner, weights, jnp.float32)
    edges = conv_edges(before, glu, after, filters)
    edges_far = swap(part_sum(2, edges, weights, jnp.bfloat16), "xh", 2, 1)
    ours_edges = part_sum(0, edges, weights, jnp.float32)
    return final(middle, ours, ours_edges, inner_far, edges_far)


def solution(mesh):
    parted = Mesh(mesh.devices.reshape(2, 8, 4, 2, 2), ("batch", "z", "y", "xh", "core"))
    in_specs = (
        P(("batch",) + CTX, TP),
        P(),
        P(None, None, TP),
        P(TP, None),
        P(),
        P(None, None, TP),
        P(None, TP),
        P(TP),
        P(TP, None),
    )
    out_specs = P(("batch",) + CTX, TP)
    return jax.shard_map(
        per_device, mesh=parted, in_specs=in_specs, out_specs=out_specs, check_vma=False
    )
```

```python
import functools
import math

import jax
import jax.numpy as jnp
from jax import lax
from jax.experimental import pallas as pl
from jax.experimental.pallas import tpu as pltpu
from jax.sharding import Mesh
from jax.sharding import PartitionSpec as P

D = 1536
HEAD = 96
HEADS_HERE = 4
COLS = 384
ROWS = 192
REACH = 15
HALO = 16
INNER = ROWS - 2 * HALO
STATS = 16
TP = ("xh", "core")
CTX = ("z", "y")
Q_SCALE = math.log2(math.e) / math.sqrt(HEAD)
VMEM_LIMIT = 8 * 2**20
OVERLAPPED = pl.CostEstimate(flops=2 * 10**10, bytes_accessed=2**20, transcendentals=0)


def layer_norm(inputs, gain, eps=1e-05):
    inputs = inputs.astype(jnp.float32)
    average = jnp.mean(inputs, axis=-1, keepdims=True)
    centered = inputs - average
    variance = jnp.mean(centered * centered, axis=-1, keepdims=True)
    return (centered * lax.rsqrt(variance + eps) * gain).astype(jnp.bfloat16)


def split_three(value):
    high = value.astype(jnp.bfloat16).astype(jnp.float32)
    rest = value - high
    mid = rest.astype(jnp.bfloat16).astype(jnp.float32)
    return high, mid, rest - mid


def head_mask(head):
    start = 128 * (head // 2)
    lane = lax.broadcasted_iota(jnp.int32, (1, 256), 1) + start
    return (lane >= head * HEAD) & (lane < (head + 1) * HEAD)


def attend(queries, keys, values, pair):
    start = 128 * pair
    window = queries[:, start : start + 256]
    masks = [head_mask(2 * pair + side) for side in range(2)]
    masked = jnp.concatenate([jnp.where(mask, window, 0) for mask in masks], 0)
    window = jnp.concatenate([block[:, start : start + 256] for block in keys], 0)
    scores = lax.dot_general(
        masked, window, (((1,), (1,)), ((), ())), preferred_element_type=jnp.float32
    )
    top = jnp.max(scores, axis=1, keepdims=True)
    weights = jnp.exp2(scores - top)
    denominator = jnp.sum(weights, axis=1, keepdims=True)
    window = jnp.concatenate([block[:, start : start + 256] for block in values], 0)
    summed = jnp.dot(weights.astype(jnp.bfloat16), window, preferred_element_type=jnp.float32)
    return masks, summed, top, denominator


def widen(part, pair):
    blank = jnp.zeros((part.shape[0], 128), jnp.float32)
    return jnp.concatenate([part, blank] if pair == 0 else [blank, part], 1)


def split_refs(refs, count):
    keys = [ref.at[:, :COLS] for ref in refs[:count]]
    values = [ref.at[:, COLS:] for ref in refs[:count]]
    return keys, values, refs[count:]


def first_attention_kernel(places, blocks, *refs):
    pieces, refs = refs[: len(places)], refs[len(places) :]
    keys, values, rest = split_refs(refs, blocks)
    o_ref, top_ref, sum_ref = rest
    lane = lax.broadcasted_iota(jnp.int32, (1, 128), 1)
    queries = [ref[at * ROWS : (at + 1) * ROWS] for ref, at in zip(pieces, places)]
    queries = jnp.concatenate(queries, 0)
    count = queries.shape[0]
    total = jnp.zeros((count, COLS), jnp.float32)
    tops = jnp.zeros((count, 128), jnp.float32)
    sums = jnp.ones((count, 128), jnp.float32)
    for pair in range(2):
        masks, summed, top, denominator = attend(queries, keys, values, pair)
        both = jnp.where(masks[0], summed[:count], jnp.where(masks[1], summed[count:], 0.0))
        total = total + widen(both, pair)
        for side in range(2):
            rows = slice(side * count, (side + 1) * count)
            tops = jnp.where(lane == 2 * pair + side, top[rows], tops)
            sums = jnp.where(lane == 2 * pair + side, denominator[rows], sums)
    o_ref[...] = total
    top_ref[...] = tops
    sum_ref[...] = sums


def last_attention_kernel(places, blocks, *refs):
    pieces, refs = refs[: len(places)], refs[len(places) :]
    keys, values, rest = split_refs(refs, blocks)
    prior_ref, top_ref, sum_ref, *outs = rest
    lane = lax.broadcasted_iota(jnp.int32, (1, 128), 1)
    queries = [ref[at * ROWS : (at + 1) * ROWS] for ref, at in zip(pieces, places)]
    queries = jnp.concatenate(queries, 0)
    count = queries.shape[0]
    tops = jnp.zeros((count, 128), jnp.float32)
    sums = jnp.zeros((count, 128), jnp.float32)
    products = []
    for pair in range(2):
        masks, summed, top, denominator = attend(queries, keys, values, pair)
        products.append((masks, summed))
        for side in range(2):
            rows = slice(side * count, (side + 1) * count)
            tops = jnp.where(lane == 2 * pair + side, top[rows], tops)
            sums = jnp.where(lane == 2 * pair + side, denominator[rows], sums)
    joint = jnp.maximum(tops, top_ref[...])
    rescale = jnp.exp2(tops - joint)
    prior_rescale = jnp.exp2(top_ref[...] - joint)
    denominator = sums * rescale + sum_ref[...] * prior_rescale
    inverse = 1.0 / denominator
    rescale = rescale * inverse
    prior_rescale = prior_rescale * inverse
    total = jnp.zeros((count, COLS), jnp.float32)
    for pair, (masks, summed) in enumerate(products):
        prior = prior_ref[:, 128 * pair : 128 * pair + 256]
        both = jnp.zeros((count, 256), jnp.float32)
        for side, mask in enumerate(masks):
            head = slice(2 * pair + side, 2 * pair + side + 1)
            part = summed[side * count : (side + 1) * count] * rescale[:, head]
            both = jnp.where(mask, part + prior * prior_rescale[:, head], both)
        total = total + widen(both, pair)
    high, mid, low = split_three(joint + jnp.log2(denominator))
    stats = jnp.where(
        lane < 4, high, jnp.where(lane < 8, pltpu.roll(mid, 4, 1), pltpu.roll(low, 8, 1))
    )
    for place, out in enumerate(outs):
        rows = slice(place * ROWS, (place + 1) * ROWS)
        out[:ROWS] = total[rows].astype(jnp.bfloat16)
        turned = jnp.concatenate([stats[rows], jnp.zeros((256 - ROWS, 128), jnp.float32)], 0)
        turned = jnp.transpose(turned)[:STATS].astype(jnp.bfloat16)
        blank = jnp.zeros((STATS, COLS - 256), jnp.bfloat16)
        out[ROWS:] = jnp.concatenate([turned, blank], 1)


def attention_cost(rows, blocks):
    flops = 2 * 2 * rows * ROWS * blocks * 256 * HEADS_HERE
    return pl.CostEstimate(flops=flops, bytes_accessed=4 * 2**20, transcendentals=0)


def first_attention(queries, blocks):
    places = tuple(at for _, at in queries)
    rows = len(places) * ROWS
    return pl.pallas_call(
        functools.partial(first_attention_kernel, places, len(blocks)),
        out_shape=[
            jax.ShapeDtypeStruct((rows, COLS), jnp.float32),
            jax.ShapeDtypeStruct((rows, 128), jnp.float32),
            jax.ShapeDtypeStruct((rows, 128), jnp.float32),
        ],
        compiler_params=pltpu.CompilerParams(vmem_limit_bytes=VMEM_LIMIT),
        cost_estimate=attention_cost(rows, len(blocks)),
        name="first_attention",
    )(*[query for query, _ in queries], *blocks)


def last_attention(queries, blocks, prior):
    places = tuple(at for _, at in queries)
    rows = len(places) * ROWS
    return pl.pallas_call(
        functools.partial(last_attention_kernel, places, len(blocks)),
        out_shape=[jax.ShapeDtypeStruct((ROWS + STATS, COLS), jnp.bfloat16)] * (rows // ROWS),
        compiler_params=pltpu.CompilerParams(vmem_limit_bytes=VMEM_LIMIT),
        cost_estimate=attention_cost(rows, len(blocks)),
        name="last_attention",
    )(*[query for query, _ in queries], *blocks, *prior)


def combine_kernel(*refs):
    parts, o_ref = refs[:4], refs[-1]
    lane = lax.broadcasted_iota(jnp.int32, (1, COLS), 1)
    logs = []
    for part in parts:
        stats = part[ROWS:, :256].astype(jnp.float32)
        logs.append(stats[0:4] + stats[4:8] + stats[8:12])
    top = functools.reduce(jnp.maximum, logs)
    shares = [jnp.exp2(log - top) for log in logs]
    inverse = 1.0 / functools.reduce(jnp.add, shares)
    shares = jnp.concatenate([share * inverse for share in shares], 0)
    blank = jnp.zeros((128 - shares.shape[0], 256), jnp.float32)
    shares = jnp.transpose(jnp.concatenate([shares, blank], 0))[:ROWS]
    total = jnp.zeros((ROWS, COLS), jnp.float32)
    for place, part in enumerate(parts):
        spread = jnp.zeros((ROWS, COLS), jnp.float32)
        for head in range(HEADS_HERE):
            inside = (lane >= head * HEAD) & (lane < (head + 1) * HEAD)
            column = place * HEADS_HERE + head
            spread = jnp.where(inside, shares[:, column : column + 1], spread)
        total = total + spread * part[:ROWS].astype(jnp.float32)
    o_ref[...] = total.astype(jnp.bfloat16)


def combine(parts, others):
    vmem = pl.BlockSpec(memory_space=pltpu.VMEM)
    anywhere = pl.BlockSpec(memory_space=pl.ANY)
    return pl.pallas_call(
        combine_kernel,
        in_specs=[vmem] * len(parts) + [anywhere] * len(others),
        out_specs=vmem,
        out_shape=jax.ShapeDtypeStruct((ROWS, COLS), jnp.bfloat16),
        compiler_params=pltpu.CompilerParams(vmem_limit_bytes=VMEM_LIMIT),
        cost_estimate=OVERLAPPED,
        name="combine",
    )(*parts, *others)


def middle_kernel(
    rows_ref, context_ref, w0, w1, w2, w3, gain_ref, glu_ref, other_ref, m_ref, g_ref, top_ref, end_ref
):
    place = lax.axis_index(TP)
    total = rows_ref[...].astype(jnp.float32)
    for offset, weight in enumerate((w0, w1, w2, w3)):
        total = total + jnp.dot(
            context_ref[place ^ offset], weight[...], preferred_element_type=jnp.float32
        )
    middle = total.astype(jnp.bfloat16)
    for position in range(4):

        @pl.when(place == position)
        def _():
            m_ref[...] = middle[:, position * COLS : (position + 1) * COLS]

    normed = layer_norm(middle, gain_ref[...].reshape(1, D))
    for half, weight in enumerate((glu_ref, other_ref)):
        value = jnp.dot(normed, weight[0], preferred_element_type=jnp.float32)
        gate = jnp.dot(normed, weight[1], preferred_element_type=jnp.float32)
        glu = (value * (1.0 / (1.0 + jnp.exp(-gate)))).astype(jnp.bfloat16)
        here = slice(half * COLS, (half + 1) * COLS)
        g_ref[:, here] = glu
        top_ref[:, here] = glu[:HALO]
        end_ref[:, here] = glu[ROWS - HALO :]


def middle_and_glu(rows, context, weights, gain, glu_weight, glu_other):
    vmem = pl.BlockSpec(memory_space=pltpu.VMEM)
    return pl.pallas_call(
        middle_kernel,
        in_specs=[vmem] * 9,
        out_specs=[vmem] * 4,
        out_shape=[
            jax.ShapeDtypeStruct((ROWS, COLS), jnp.bfloat16),
            jax.ShapeDtypeStruct((ROWS, 2 * COLS), jnp.bfloat16),
            jax.ShapeDtypeStruct((HALO, 2 * COLS), jnp.bfloat16),
            jax.ShapeDtypeStruct((HALO, 2 * COLS), jnp.bfloat16),
        ],
        compiler_params=pltpu.CompilerParams(vmem_limit_bytes=VMEM_LIMIT),
        cost_estimate=OVERLAPPED,
        name="middle",
    )(rows, context, *weights, gain, glu_weight, glu_other)


def convolve(held, filters, count, store):
    for half, (taps_ref, bias_ref) in enumerate(filters):
        taps = taps_ref[...].astype(jnp.float32)
        for column in range(COLS // 128):
            local = slice(column * 128, (column + 1) * 128)
            here = slice(half * COLS + column * 128, half * COLS + (column + 1) * 128)
            total = jnp.zeros((count, 128), jnp.float32) + bias_ref[local].reshape(1, 128)
            for offset in range(8):
                group = jnp.zeros((count + 8, 128), jnp.float32)
                for begin in range(offset, 2 * HALO, 8):
                    tap = begin - (HALO - REACH)
                    if tap >= 0:
                        aligned = held[begin - offset : begin - offset + count + 8, here]
                        group = group + aligned * taps[tap : tap + 1, local]
                total = total + group[offset : offset + count]
            store(here, (total / (1.0 + jnp.exp(-total))).astype(jnp.bfloat16))


def inner_kernel(glu_ref, taps0, bias0, taps1, bias1, o_ref, held):
    held[...] = glu_ref[...].astype(jnp.float32)

    def store(here, value):
        o_ref[:, here] = value

    convolve(held, ((taps0, bias0), (taps1, bias1)), INNER, store)


def edges_kernel(before_ref, glu_ref, after_ref, taps0, bias0, taps1, bias1, w_own, w_other, o_ref, far_ref, held):
    for side in range(2):
        if side == 0:
            held[:HALO] = before_ref[...].astype(jnp.float32)
            held[HALO:] = glu_ref[: 2 * HALO].astype(jnp.float32)
        else:
            held[: 2 * HALO] = glu_ref[ROWS - 2 * HALO :].astype(jnp.float32)
            held[2 * HALO :] = after_ref[...].astype(jnp.float32)

        def store(here, value):
            o_ref[side * HALO : (side + 1) * HALO, here] = value

        convolve(held, ((taps0, bias0), (taps1, bias1)), HALO, store)
    far_ref[...] = product(2, o_ref, w_own, w_other).astype(jnp.bfloat16)


def conv_inner(glu, filters):
    return pl.pallas_call(
        inner_kernel,
        out_shape=jax.ShapeDtypeStruct((INNER, 2 * COLS), jnp.bfloat16),
        scratch_shapes=[pltpu.VMEM((ROWS, 2 * COLS), jnp.float32)],
        compiler_params=pltpu.CompilerParams(vmem_limit_bytes=VMEM_LIMIT),
        name="inner",
    )(glu, *filters)


def conv_edges(before, glu, after, filters, weights):
    return pl.pallas_call(
        edges_kernel,
        out_shape=[
            jax.ShapeDtypeStruct((2 * HALO, 2 * COLS), jnp.bfloat16),
            jax.ShapeDtypeStruct((2 * HALO, COLS), jnp.bfloat16),
        ],
        scratch_shapes=[pltpu.VMEM((3 * HALO, 2 * COLS), jnp.float32)],
        compiler_params=pltpu.CompilerParams(vmem_limit_bytes=VMEM_LIMIT),
        cost_estimate=OVERLAPPED,
        name="edges",
    )(before, glu, after, *filters, *weights)


def project_kernel(eps_ref, rows_ref, gain_ref, w_ref, kv_ref, q_ref):
    normed = layer_norm(rows_ref[...], gain_ref[...].reshape(1, D), eps_ref[0:1, 0:1])
    for half in range(2):
        kv_ref[:, half * COLS : (half + 1) * COLS] = jnp.dot(
            normed, w_ref[1 + half], preferred_element_type=jnp.float32
        ).astype(jnp.bfloat16)
    query = jnp.dot(normed, w_ref[0], preferred_element_type=jnp.float32)
    q_ref[...] = (query * Q_SCALE).astype(jnp.bfloat16)


def project(eps, rows, gain, weights):
    return pl.pallas_call(
        project_kernel,
        out_shape=[
            jax.ShapeDtypeStruct((ROWS, 2 * COLS), jnp.bfloat16),
            jax.ShapeDtypeStruct((ROWS, COLS), jnp.bfloat16),
        ],
        compiler_params=pltpu.CompilerParams(vmem_limit_bytes=VMEM_LIMIT),
        name="project",
    )(eps, rows, gain, weights)


def epsilon_kernel(o_ref):
    o_ref[...] = jnp.full((8, 128), 1e-05, jnp.float32)


def epsilon():
    return pl.pallas_call(
        epsilon_kernel,
        out_shape=jax.ShapeDtypeStruct((8, 128), jnp.float32),
        compiler_params=pltpu.CompilerParams(vmem_limit_bytes=VMEM_LIMIT),
        cost_estimate=OVERLAPPED,
        name="epsilon",
    )()


def join_kernel(a_ref, b_ref, _, o_ref):
    o_ref[:ROWS] = a_ref[...]
    o_ref[ROWS:] = b_ref[...]


def join(a, b, other):
    vmem = pl.BlockSpec(memory_space=pltpu.VMEM)
    return pl.pallas_call(
        join_kernel,
        in_specs=[vmem, vmem, pl.BlockSpec(memory_space=pl.ANY)],
        out_shape=jax.ShapeDtypeStruct((2 * ROWS, COLS), jnp.bfloat16),
        compiler_params=pltpu.CompilerParams(vmem_limit_bytes=VMEM_LIMIT),
        name="join",
    )(a, b, other)


def halves_kernel(a_ref, b_ref, _, a_out, b_out):
    a_out[...] = a_ref[: ROWS // 2]
    b_out[...] = b_ref[ROWS // 2 :]


def halves(a, b, other):
    vmem = pl.BlockSpec(memory_space=pltpu.VMEM)
    return pl.pallas_call(
        halves_kernel,
        in_specs=[vmem, vmem, pl.BlockSpec(memory_space=pl.ANY)],
        out_shape=[jax.ShapeDtypeStruct((ROWS // 2, 2 * COLS), jnp.bfloat16)] * 2,
        compiler_params=pltpu.CompilerParams(vmem_limit_bytes=VMEM_LIMIT),
        name="halves",
    )(a, b, other)


def product(flip, act_ref, w_own, w_other):
    columns = pl.ds(pl.multiple_of((lax.axis_index(TP) ^ flip) * COLS, 128), COLS)
    total = jnp.dot(act_ref[:, :COLS], w_own[:, columns], preferred_element_type=jnp.float32)
    return total + jnp.dot(
        act_ref[:, COLS:], w_other[:, columns], preferred_element_type=jnp.float32
    )


def part_kernel(flip, act_ref, w_own, w_other, o_ref):
    o_ref[...] = product(flip, act_ref, w_own, w_other).astype(o_ref.dtype)


def part_sum(flip, act, weights, kind):
    return pl.pallas_call(
        functools.partial(part_kernel, flip),
        out_shape=jax.ShapeDtypeStruct((act.shape[0], COLS), kind),
        compiler_params=pltpu.CompilerParams(vmem_limit_bytes=VMEM_LIMIT),
        name="part_sum",
    )(act, *weights)


def final_kernel(middle_ref, ours_ref, ours_edges_ref, inner_ref, edges_ref, o_ref):
    here = slice(HALO, HALO + INNER)
    total = ours_ref[...] + inner_ref[...].astype(jnp.float32)
    o_ref[here] = (middle_ref[here].astype(jnp.float32) + total).astype(jnp.bfloat16)
    total = ours_edges_ref[...] + edges_ref[...].astype(jnp.float32)
    for side in range(2):
        here = slice(side * (ROWS - HALO), side * (ROWS - HALO) + HALO)
        part = total[side * HALO : (side + 1) * HALO]
        o_ref[here] = (middle_ref[here].astype(jnp.float32) + part).astype(jnp.bfloat16)


def final(middle, ours, ours_edges, inner, edges):
    return pl.pallas_call(
        final_kernel,
        out_shape=jax.ShapeDtypeStruct((ROWS, COLS), jnp.bfloat16),
        compiler_params=pltpu.CompilerParams(vmem_limit_bytes=VMEM_LIMIT),
        name="final",
    )(middle, ours, ours_edges, inner, edges)


def swap(value, axis, count, flip):
    return lax.ppermute(value, axis, [(i, i ^ flip) for i in range(count)])


def shift(value, axis, count, offset):
    return lax.ppermute(value, axis, [(i, (i + offset) % count) for i in range(count)])


def per_device(
    frames,
    attn_gain,
    query_key_value,
    out_weight,
    conv_gain,
    glu_weight,
    depth_kernel,
    depth_bias,
    proj_weight,
):
    out_core = swap(out_weight, "core", 2, 1)
    glu_core = swap(glu_weight, "core", 2, 1)
    out_far = swap(out_weight, "xh", 2, 1)
    whole_rows = lax.all_gather(frames, TP, axis=1, tiled=True)
    mine, query = project(epsilon(), whole_rows, attn_gain, query_key_value)
    lower1, upper1 = shift(mine, "z", 8, 1), shift(mine, "z", 8, -1)
    query1 = swap(query, "y", 4, 1)
    lower2, upper2 = shift(lower1, "z", 8, 1), shift(upper1, "z", 8, -1)
    pair2 = swap(join(query, query1, out_core), "y", 4, 2)
    low_half, high_half = halves(lower2, upper2, glu_core)
    second = [
        shift(lower2, "z", 8, 1),
        shift(upper2, "z", 8, -1),
        shift(low_half, "z", 8, 2),
        shift(high_half, "z", 8, -2),
    ]
    blocks = [mine, lower1, upper1, lower2, upper2]
    groups = ([(pair2, 0)], [(query1, 0), (pair2, 1)], [(query, 0)])
    priors = [first_attention(group, blocks) for group in groups]
    (partial2,) = last_attention(groups[0], second, priors[0])
    part2 = swap(partial2, "y", 4, 2)
    partial1, partial3 = last_attention(groups[1], second, priors[1])
    part1, part3 = swap(partial1, "y", 4, 1), swap(partial3, "y", 4, 3)
    (partial0,) = last_attention(groups[2], second, priors[2])
    out_far_core = swap(out_far, "core", 2, 1)
    out_pieces = (out_weight, out_core, out_far, out_far_core)
    taps_core = swap(depth_kernel, "core", 2, 1)
    bias_core = swap(depth_bias, "core", 2, 1)
    context = combine([partial0, part1, part2, part3], [taps_core, bias_core])
    proj_core = swap(proj_weight, "core", 2, 1)
    context = lax.all_gather(context, TP, axis=0, tiled=False)
    middle, glu, top, end = middle_and_glu(
        whole_rows, context, out_pieces, conv_gain, glu_weight, glu_core
    )
    before = lax.ppermute(end, CTX, [(i, i + 1) for i in range(31)])
    after = lax.ppermute(top, CTX, [(i + 1, i) for i in range(31)])
    weights = (proj_weight, proj_core)
    filters = (depth_kernel, depth_bias, taps_core, bias_core)
    inner = conv_inner(glu, filters)
    inner_far = swap(part_sum(2, inner, weights, jnp.bfloat16), "xh", 2, 1)
    ours = part_sum(0, inner, weights, jnp.float32)
    edges, edges_far = conv_edges(before, glu, after, filters, weights)
    edges_far = swap(edges_far, "xh", 2, 1)
    ours_edges = part_sum(0, edges, weights, jnp.float32)
    return final(middle, ours, ours_edges, inner_far, edges_far)


def solution(mesh):
    parted = Mesh(mesh.devices.reshape(2, 8, 4, 2, 2), ("batch", "z", "y", "xh", "core"))
    in_specs = (
        P(("batch",) + CTX, TP),
        P(),
        P(None, None, TP),
        P(TP, None),
        P(),
        P(None, None, TP),
        P(None, TP),
        P(TP),
        P(TP, None),
    )
    out_specs = P(("batch",) + CTX, TP)
    return jax.shard_map(
        per_device, mesh=parted, in_specs=in_specs, out_specs=out_specs, check_vma=False
    )
```
